128 devices in a mesh: dom: 32 (over y, x, core), esplit: 4 (over z).
Axes of the slice: x: 4, y: 4, z: 4, core: 2. Of those that a mesh axis runs over, the one named last changes fastest.
Arguments:
- features: bfloat16 [524288, 128], P('dom'), may hold values from -6 to 6
- adjacency: bfloat16 [32, 4, 16, 128, 32, 128], P('dom', 'esplit'), as said below
- tile_source: int32 [32, 4, 16, 32], P('dom', 'esplit'), may hold values from 0 to 287, as said below
- hub_rows: int32 [32, 512], P('dom'), may hold values from 0 to 16383, as said below
- send_rows: int32 [32, 32, 128], P('dom'), may hold values from 0 to 16383, as said below
- send_live: int32 [32, 32], P('dom'), may hold values from 32 to 128, as said below
- target_block: int32 [32], P('dom'), may hold values from 0 to 112
- w_self: bfloat16 [128, 128], replicated, may hold values from -0.5 to 0.5
- w_neigh: bfloat16 [128, 128], replicated, may hold values from -2 to 2
- out_bias: bfloat16 [128], replicated, may hold values from -3 to 3
- out_grad: bfloat16 [65536, 128], P('dom'), may hold values from -6 to 6
Outputs:
- layer_out: bfloat16 [65536, 128], P(('dom', 'esplit'))
- grad_features: float32 [524288, 128], P(('dom', 'esplit'))
- grad_w_self: float32 [128, 128], replicated
- grad_w_neigh: float32 [128, 128], replicated
- grad_bias: float32 [128], replicated
The draws below stay inside these ranges and needn't reach their ends.
Inputs may be any that keep to these rules, and one draw needn't show every extreme that they name: `adjacency`: nonnegative edge weights, zero where a tile holds no edge. `tile_source`: a block index into the partition's source table. `hub_rows`: distinct local rows within each partition. `send_rows`: local rows of the sending partition, distinct within each list. `send_live`: in each sender's lists one reaches 128.
All inputs are finite; a program needn't handle non-finite values.
Results may differ from the reference program's by a relative error of at most 0.00045.
Values may be sent and summed in bfloat16 or wider, within the bound.
A program may use at most 256 MiB of HBM per device.

```python
import math
import jax
import jax.numpy as jnp
from jax import lax

F = 128
BLK = 128
ROWS = 16384
KE = 32
HUB_DEV = 512
HALO_PEER = 128
TGT = 2048
TB = 16
HUBS = 16384
TARGETS = 65536
NODES = 524288
SRC_BLOCKS = 288
N_DOM = 32
N_ESPLIT = 4


def draw_adjacency(key, part):
    key = jax.random.fold_in(key, 11)
    split_share = (1.0 + jnp.arange(N_ESPLIT, dtype=jnp.float32)) / (N_ESPLIT * (N_ESPLIT + 1) / 2.0)
    tile_shape = (N_ESPLIT, TB, BLK, KE, BLK)

    def one_domain(dom_key):
        rate_key, mask_key, weight_key = jax.random.split(dom_key, 3)
        row_density = jnp.exp(jax.random.uniform(rate_key, (1, TB, BLK, 1, 1), jnp.float32, math.log(0.004), math.log(0.12)))
        chance = jnp.minimum(row_density * split_share[:, None, None, None, None] * N_ESPLIT, 1.0)
        edge_hit = jax.random.uniform(mask_key, tile_shape, jnp.float32) < chance
        weights = jnp.exp(jax.random.uniform(weight_key, tile_shape, jnp.float32, math.log(0.5), math.log(2.0)))
        return jnp.where(edge_hit, weights, 0.0).astype(jnp.bfloat16)
    return lax.map(one_domain, jax.random.split(key, N_DOM))


def draw_tile_source(key, part):
    key = jax.random.fold_in(key, 12)
    region_key, own_key, hub_key, halo_key = jax.random.split(key, 4)
    tile_shape = (N_DOM, N_ESPLIT, TB, KE)
    region = jax.random.randint(region_key, tile_shape, 0, 4)
    own_block = jax.random.randint(own_key, tile_shape, 0, ROWS // BLK)
    hub_block = ROWS // BLK + jax.random.randint(hub_key, tile_shape, 0, HUBS // BLK)
    halo_block = (ROWS + HUBS) // BLK + jax.random.randint(halo_key, tile_shape, 0, N_DOM * HALO_PEER // BLK)
    chosen = jnp.where(region < 2, hub_block, jnp.where(region == 2, own_block, halo_block))
    chosen = chosen.at[0, 0, 0, 0].set(0).at[N_DOM - 1, N_ESPLIT - 1, TB - 1, KE - 1].set(SRC_BLOCKS - 1)
    return chosen.astype(jnp.int32)


def draw_hub_rows(key, part):
    key = jax.random.fold_in(key, 13)

    def one_owner(one_key):
        return jax.random.permutation(one_key, ROWS)[:HUB_DEV]
    return jax.vmap(one_owner)(jax.random.split(key, N_DOM)).astype(jnp.int32)


def draw_send_rows(key, part):
    key = jax.random.fold_in(key, 14)

    def one_list(one_key):
        return jax.random.permutation(one_key, ROWS)[:HALO_PEER]
    picked = jax.vmap(one_list)(jax.random.split(key, N_DOM * N_DOM))
    return picked.reshape(N_DOM, N_DOM, HALO_PEER).astype(jnp.int32)


def draw_send_live(key, part):
    key = jax.random.fold_in(key, 15)
    count_key, peer_key = jax.random.split(key, 2)
    counts = jax.random.randint(count_key, (N_DOM, N_DOM), HALO_PEER // 4, HALO_PEER + 1)
    fullest = jax.random.randint(peer_key, (N_DOM, 1), 0, N_DOM)
    counts = jnp.where(jnp.arange(N_DOM)[None, :] == fullest, HALO_PEER, counts)
    return counts.astype(jnp.int32)


def touch_ends(values, key, smallest, largest):
    extent = values.shape
    place = [jax.random.randint(jax.random.fold_in(key, axis), (), 0, extent[axis]) for axis in range(len(extent))]
    values = values.at[tuple(place)].set(smallest)
    longest = extent.index(max(extent))
    place[longest] = (place[longest] + 1) % extent[longest]
    return values.at[tuple(place)].set(largest)


def steps_of(key, shape, shards, smallest, largest):
    def one(axis_at, parts):
        steps = jax.random.uniform(jax.random.fold_in(jax.random.fold_in(key, 6), axis_at), (parts,), jnp.float32, smallest / len(shards), largest / len(shards))
        return jnp.repeat(jnp.exp(steps), shape[axis_at] // parts).reshape((-1,) + (1,) * (len(shape) - axis_at - 1))

    factor_of = one(*shards[0])
    for cut in shards[1:]:
        factor_of = factor_of * one(*cut)
    return factor_of


def scatter_about(key, dims, spread, limit, shards=(), kind=jnp.bfloat16):
    values = jax.random.normal(key, dims, jnp.float32) * spread
    if len(shards) > 0:
        values = steps_of(key, dims, shards, -0.22, 0.18) * values
    return jnp.clip(values, min=-limit, max=limit).astype(kind)


def setup_inputs(seed: int = 0) -> dict:
    seeds = jax.random.split(jax.random.key(seed), 12)
    return {
        "features": scatter_about(seeds[0], (NODES, F), 1.0, 6.0, ((0, 32),)),
        "adjacency": draw_adjacency(jax.random.fold_in(seeds[11], 71), 0),
        "tile_source": draw_tile_source(jax.random.fold_in(seeds[11], 71), 0),
        "hub_rows": draw_hub_rows(jax.random.fold_in(seeds[11], 71), 0),
        "send_rows": draw_send_rows(jax.random.fold_in(seeds[11], 71), 0),
        "send_live": draw_send_live(jax.random.fold_in(seeds[11], 71), 0),
        "target_block": touch_ends(jax.random.randint(seeds[6], (N_DOM,), 0, (ROWS - TGT) // BLK + 1), jax.random.fold_in(seeds[6], 1), 0, ((ROWS - TGT) // BLK + 1) - 1).astype(jnp.int32),
        "w_self": scatter_about(seeds[7], (F, F), F ** -0.5, 0.5),
        "w_neigh": scatter_about(seeds[8], (F, F), (F // 16) ** -0.5, 2.0),
        "out_bias": scatter_about(seeds[9], (F,), 0.5, 3.0),
        "out_grad": scatter_about(seeds[10], (TARGETS, F), 1.0, 6.0, ((0, 32),)),
    }


def one_partition(own_rows, hub_table, halo_rows, adjacency_part, sources_part, first_block, grads_part, w_self, w_neigh, out_bias):
    highest = lax.Precision.HIGHEST
    source_table = jnp.concatenate([own_rows, hub_table, halo_rows], axis=0)
    source_blocks = source_table.reshape(SRC_BLOCKS, BLK, F)[sources_part]
    tile_vals = adjacency_part.astype(jnp.float32)
    numerator = jnp.einsum('ebikj,ebkjf->bif', tile_vals, source_blocks.astype(jnp.float32), precision=highest).reshape(TGT, F)
    degree = lax.optimization_barrier(jnp.sum(tile_vals, axis=(0, 3, 4))).reshape(TGT)
    divisor = jnp.maximum(degree, 1.0)[:, None]
    aggregate = numerator / divisor
    start_row = (first_block * BLK).astype(jnp.int32)
    self_rows = lax.dynamic_slice_in_dim(own_rows, start_row, TGT, 0)
    grads_wide = grads_part.astype(jnp.float32)
    layer_out = (jnp.dot(aggregate, w_neigh.astype(jnp.float32), precision=highest) + jnp.dot(self_rows, w_self, preferred_element_type=jnp.float32) + out_bias.astype(jnp.float32)).astype(jnp.bfloat16)
    numer_grad = jnp.dot(grads_wide, w_neigh.astype(jnp.float32).T, precision=highest) / divisor
    contrib = jnp.einsum('ebikj,bif->ebkjf', tile_vals, numer_grad.reshape(TB, BLK, F), precision=highest)
    grad_table = jnp.zeros((SRC_BLOCKS, BLK, F), jnp.float32).at[sources_part].add(contrib).reshape(SRC_BLOCKS * BLK, F)
    own_grad = grad_table[:ROWS]
    self_grad = lax.dynamic_slice_in_dim(own_grad, start_row, TGT, 0) + jnp.dot(grads_part, w_self.T, preferred_element_type=jnp.float32)
    own_grad = lax.dynamic_update_slice_in_dim(own_grad, self_grad, start_row, 0)
    neigh_wgrad = jnp.dot(aggregate.T, grads_wide, precision=highest)
    self_wgrad = jnp.dot(self_rows.T, grads_part, preferred_element_type=jnp.float32)
    bias_grad = lax.optimization_barrier(jnp.sum(grads_wide, axis=0))
    hub_grad = grad_table[ROWS:ROWS + HUBS]
    halo_grad = grad_table[ROWS + HUBS:].reshape(N_DOM, HALO_PEER, F)
    return (layer_out, own_grad, hub_grad, halo_grad, neigh_wgrad, self_wgrad, bias_grad)

def reference(features, adjacency, tile_source, hub_rows, send_rows, send_live, target_block, w_self, w_neigh, out_bias, out_grad):
    own_all = features.reshape(N_DOM, ROWS, F)
    owners = jnp.arange(N_DOM, dtype=jnp.int32)
    hub_table = own_all[owners[:, None], hub_rows].reshape(HUBS, F)
    slot_live = jnp.arange(HALO_PEER, dtype=jnp.int32)[None, None, :] < send_live[:, :, None]
    halo_all = jnp.where(slot_live[:, :, :, None], own_all[owners[:, None, None], send_rows], jnp.zeros((), features.dtype))
    halo_by_target = jnp.swapaxes(halo_all, 0, 1).reshape(N_DOM, N_DOM * HALO_PEER, F)
    grads_all = out_grad.reshape(N_DOM, TGT, F)

    def per_partition(inputs):
        own_rows, halo_rows, adjacency_part, sources_part, first_block, grads_part = inputs
        return one_partition(own_rows, hub_table, halo_rows, adjacency_part, sources_part, first_block, grads_part, w_self, w_neigh, out_bias)
    results = lax.map(per_partition, (own_all, halo_by_target, adjacency, tile_source, target_block, grads_all))
    layer_out, own_grad, hub_grad, halo_grad, neigh_wgrad, self_wgrad, bias_grad = results
    hub_total = lax.optimization_barrier(jnp.sum(hub_grad, axis=0)).reshape(N_DOM, HUB_DEV, F)
    own_grad = own_grad.at[owners[:, None], hub_rows].add(hub_total)
    halo_back = jnp.where(slot_live[:, :, :, None], jnp.swapaxes(halo_grad, 0, 1), 0.0)
    own_grad = own_grad.at[owners[:, None, None], send_rows].add(halo_back)
    norm_scale = math.sqrt(TARGETS)
    return (layer_out.reshape(TARGETS, F), own_grad.reshape(NODES, F), lax.optimization_barrier(jnp.sum(self_wgrad, axis=0)) / norm_scale, lax.optimization_barrier(jnp.sum(neigh_wgrad, axis=0)) / norm_scale, lax.optimization_barrier(jnp.sum(bias_grad, axis=0)) / norm_scale)
```

```python
import math

import jax
import jax.numpy as jnp
from jax import lax
from jax.experimental import pallas as pl
from jax.experimental.pallas import tpu as pltpu
from jax.sharding import PartitionSpec as P

F32 = jnp.float32
BF16 = jnp.bfloat16
VMEM_LIMIT = 56 * 2**20
ANY = pl.BlockSpec(memory_space=pl.ANY)
SMEM = pl.BlockSpec(memory_space=pltpu.SMEM)
VMEM = pl.BlockSpec(memory_space=pltpu.VMEM)
PARAMS = pltpu.CompilerParams(vmem_limit_bytes=VMEM_LIMIT)


def block_copy(src, dst, sem, block):
    return pltpu.make_async_copy(src.at[block], dst.at[block], sem.at[block])


def degree_body(adj, deg, buf, sem):
    blocks = adj.shape[0]
    for b in range(blocks):
        block_copy(adj, buf, sem, b).start()

    @pl.loop(0, blocks)
    def _(b):
        block_copy(adj, buf, sem, b).wait()
        by_column = jnp.sum(buf[b].astype(F32), axis=1)
        deg[b] = lax.dot_general(
            jnp.ones((8, by_column.shape[1]), F32),
            by_column,
            (((1,), (1,)), ((), ())),
            precision=lax.Precision.HIGHEST,
            preferred_element_type=F32,
        )


def degree_part(adj):
    blocks, rows, _, _ = adj.shape
    return pl.pallas_call(
        degree_body,
        in_specs=[ANY],
        out_specs=VMEM,
        out_shape=jax.ShapeDtypeStruct((blocks, 8, rows), F32),
        scratch_shapes=[pltpu.VMEM(adj.shape, BF16), pltpu.SemaphoreType.DMA((blocks,))],
        compiler_params=PARAMS,
    )(adj)


def split_slots(tiles, adj_block):
    rows = adj_block.shape[0]
    for g in range(rows // 16):
        tiles[:, pl.ds(g * 16, 16), :] = jnp.swapaxes(adj_block[pl.ds(g * 16, 16)], 0, 1)


def backward_body(src, adj, grads, w_neigh, deg, table_out, table, buf, tiles, sem, out_sem):
    blocks, rows, slots, _ = adj.shape
    for b in range(blocks):
        block_copy(adj, buf, sem, b).start()

    @pl.loop(0, table.shape[0], unroll=8)
    def _(c):
        table[c] = jnp.zeros(table.shape[1:], F32)

    @pl.loop(0, blocks)
    def _(b):
        block_copy(adj, buf, sem, b).wait()
        split_slots(tiles, buf.at[b])
        grad_t = lax.dot_general(
            w_neigh[...],
            grads[pl.ds(pl.multiple_of(b * rows, rows), rows), :],
            (((1,), (1,)), ((), ())),
            preferred_element_type=F32,
        )
        grad_t = grad_t / jnp.maximum(deg[b][0:1], 1.0)
        high = grad_t.astype(BF16)
        low = (grad_t - high.astype(F32)).astype(BF16)
        both = jnp.concatenate([high, low], axis=1)
        for k in range(0, slots, 2):
            pair = jnp.concatenate([tiles[k], tiles[k + 1]], axis=1)
            part = jnp.dot(both, jnp.concatenate([pair, pair], axis=0), preferred_element_type=F32)
            table[src[b, k]] += part[:, : part.shape[1] // 2]
            table[src[b, k + 1]] += part[:, part.shape[1] // 2 :]

    @pl.loop(0, table.shape[0], unroll=4)
    def _(c):
        table[c] = table[c].T

    copy = pltpu.make_async_copy(table, table_out, out_sem)
    copy.start()
    copy.wait()


def backward(src, adj, grads, w_neigh, deg, table_blocks):
    blocks, rows, slots, cols = adj.shape
    feat = grads.shape[1]
    return pl.pallas_call(
        backward_body,
        in_specs=[SMEM, ANY, VMEM, VMEM, VMEM],
        out_specs=ANY,
        out_shape=jax.ShapeDtypeStruct((table_blocks, cols, feat), F32),
        scratch_shapes=[
            pltpu.VMEM((table_blocks, feat, cols), F32),
            pltpu.VMEM(adj.shape, BF16),
            pltpu.VMEM((slots, rows, cols), BF16),
            pltpu.SemaphoreType.DMA((blocks,)),
            pltpu.SemaphoreType.DMA,
        ],
        compiler_params=PARAMS,
    )(src, adj, grads, w_neigh, deg)


def forward_body(src, adj, own, hub, halo, num, table, buf, tiles, sem, table_sem):
    blocks, rows, slots, _ = adj.shape
    copies = []
    start = 0
    for i, part in enumerate((own, hub, halo)):
        count = part.shape[0]
        copies.append(pltpu.make_async_copy(part, table.at[pl.ds(start, count)], table_sem.at[i]))
        start += count
    for copy in copies:
        copy.start()
    for b in range(blocks):
        block_copy(adj, buf, sem, b).start()
    for copy in copies:
        copy.wait()

    @pl.loop(0, blocks)
    def _(b):
        block_copy(adj, buf, sem, b).wait()
        split_slots(tiles, buf.at[b])
        total = jnp.zeros((rows, num.shape[1]), F32)
        for k in range(0, slots, 2):
            pair = jnp.concatenate([tiles[k], tiles[k + 1]], axis=1)
            rhs = jnp.concatenate([table[src[b, k]], table[src[b, k + 1]]], axis=0)
            total = total + jnp.dot(pair, rhs, preferred_element_type=F32)
        num[pl.ds(pl.multiple_of(b * rows, rows), rows), :] = total


def forward(src, adj, own, hub, halo):
    blocks, rows, slots, cols = adj.shape
    table_blocks = own.shape[0] + hub.shape[0] + halo.shape[0]
    feat = own.shape[2]
    return pl.pallas_call(
        forward_body,
        in_specs=[SMEM, ANY, ANY, ANY, ANY],
        out_specs=VMEM,
        out_shape=jax.ShapeDtypeStruct((blocks * rows, feat), F32),
        scratch_shapes=[
            pltpu.VMEM((table_blocks, cols, feat), BF16),
            pltpu.VMEM(adj.shape, BF16),
            pltpu.VMEM((slots, rows, cols), BF16),
            pltpu.SemaphoreType.DMA((blocks,)),
            pltpu.SemaphoreType.DMA((3,)),
        ],
        compiler_params=PARAMS,
    )(src, adj, own, hub, halo)


def local(
    features,
    adjacency,
    tile_source,
    hub_rows,
    send_rows,
    send_live,
    target_block,
    w_self,
    w_neigh,
    out_bias,
    out_grad,
):
    highest = lax.Precision.HIGHEST
    own_count, feat = features.shape
    peers = lax.axis_size("dom")
    shares = lax.axis_size("esplit")
    share = lax.axis_index("esplit")
    adj = adjacency[0, 0]
    src = tile_source[0, 0]
    blocks, rows, _, cols = adj.shape
    targets = blocks * rows
    quarter = targets // shares
    hub_idx = hub_rows[0]
    hubs = hub_idx.shape[0]
    lists = send_rows[0]
    slots = lists.shape[1]
    live = jnp.arange(slots, dtype=jnp.int32)[None, :] < send_live[0][:, None]

    hub_local = features[hub_idx]
    halo_send = jnp.where(live[:, :, None], features[lists], jnp.zeros((), features.dtype))
    hub_all = lax.all_gather(hub_local, "dom", axis=0, tiled=True)
    halo_all = lax.all_to_all(halo_send, "dom", split_axis=0, concat_axis=0, tiled=True)

    deg = lax.psum(degree_part(adj)[:, :1], "esplit")
    table_blocks = (own_count + peers * (hubs + slots)) // cols
    deg_rows = jnp.broadcast_to(deg, (blocks, 8, rows))
    table_grad = backward(src, adj, out_grad, w_neigh, deg_rows, table_blocks).reshape(-1, feat)
    own_grad = table_grad[:own_count]
    hub_grad = table_grad[own_count : own_count + peers * hubs].reshape(peers, hubs, feat)
    halo_grad = table_grad[own_count + peers * hubs :].reshape(peers, slots, feat)
    packet = jnp.concatenate([hub_grad, halo_grad], axis=1)
    returned = lax.all_to_all(packet, "dom", split_axis=0, concat_axis=0, tiled=True)

    numerator = forward(
        src,
        adj,
        features.reshape(-1, cols, feat),
        hub_all.reshape(-1, cols, feat),
        halo_all.reshape(-1, cols, feat),
    )
    num = lax.psum_scatter(numerator, "esplit", scatter_dimension=0, tiled=True)

    start_row = target_block[0] * rows
    first = share * quarter
    self_start = start_row + first
    self_rows = lax.dynamic_slice_in_dim(features, self_start, quarter, 0)
    grads = lax.dynamic_slice_in_dim(out_grad, first, quarter, 0)
    grads_wide = grads.astype(F32)
    divisor = jnp.maximum(lax.dynamic_slice_in_dim(deg.reshape(targets), first, quarter, 0), 1.0)
    aggregate = num / divisor[:, None]
    layer_out = (
        jnp.dot(aggregate, w_neigh.astype(F32), precision=highest)
        + jnp.dot(self_rows, w_self, preferred_element_type=F32)
        + out_bias.astype(F32)
    ).astype(BF16)
    contract = (((0,), (0,)), ((), ()))
    weight_grads = jnp.concatenate(
        [
            lax.dot_general(self_rows, grads, contract, preferred_element_type=F32),
            lax.dot_general(aggregate, grads_wide, contract, precision=highest),
            jnp.broadcast_to(jnp.sum(grads_wide, axis=0)[None, :], (8, feat)),
        ],
        axis=0,
    )
    weight_grads = lax.psum(weight_grads, ("dom", "esplit")) / math.sqrt(targets * peers)

    self_grad = lax.dynamic_slice_in_dim(own_grad, self_start, quarter, 0) + jnp.dot(
        grads, w_self.T, preferred_element_type=F32
    )
    own_grad = lax.dynamic_update_slice_in_dim(own_grad, self_grad, self_start, 0)
    own_grad = own_grad.at[hub_idx].add(jnp.sum(returned[:, :hubs], axis=0))
    own_grad = own_grad.at[lists].add(jnp.where(live[:, :, None], returned[:, hubs:], 0.0))
    grad_features = lax.psum_scatter(own_grad, "esplit", scatter_dimension=0, tiled=True)
    return (
        layer_out,
        grad_features,
        weight_grads[:feat],
        weight_grads[feat : 2 * feat],
        weight_grads[2 * feat],
    )


def solution(mesh):
    in_specs = (
        P("dom", None),
        P("dom", "esplit", None, None, None, None),
        P("dom", "esplit", None, None),
        P("dom", None),
        P("dom", None, None),
        P("dom", None),
        P("dom"),
        P(),
        P(),
        P(),
        P("dom", None),
    )
    out_specs = (P(("dom", "esplit"), None), P(("dom", "esplit"), None), P(), P(), P())
    return jax.shard_map(local, mesh=mesh, in_specs=in_specs, out_specs=out_specs, check_vma=False)
```

```python
import math

import jax
import jax.numpy as jnp
from jax import lax
from jax.experimental import pallas as pl
from jax.experimental.pallas import tpu as pltpu
from jax.sharding import PartitionSpec as P

F32 = jnp.float32
BF16 = jnp.bfloat16
I16 = jnp.int16
I32 = jnp.int32
MESH = pl.DeviceIdType.MESH
DMA = pltpu.SemaphoreType.DMA
VMEM_LIMIT = 56 * 2**20
ANY = pl.BlockSpec(memory_space=pl.ANY)
SMEM = pl.BlockSpec(memory_space=pltpu.SMEM)
VMEM = pl.BlockSpec(memory_space=pltpu.VMEM)
PARAMS = pltpu.CompilerParams(vmem_limit_bytes=VMEM_LIMIT)
BLK = 128
TOP = 32767.0


def remote_params(number):
    return pltpu.CompilerParams(
        vmem_limit_bytes=VMEM_LIMIT, collective_id=number, has_side_effects=True
    )


class Place:
    def __init__(self):
        self.d = lax.axis_index("dom")
        self.z = lax.axis_index("esplit")
        self.core = lax.rem(self.d, 2)
        self.x = lax.rem(lax.div(self.d, 2), 4)
        self.y = lax.div(self.d, 8)

    def at(self, axis):
        return {"x": self.x, "y": self.y, "z": self.z}[axis]

    def step(self, axis, by):
        return lax.rem(self.at(axis) + (by + 4), 4)

    def device(self, axis, by):
        if axis == "core":
            return (self.d + 1 - 2 * self.core, self.z)
        there = self.step(axis, by)
        if axis == "z":
            return (self.d, there)
        if axis == "x":
            return ((self.y * 4 + there) * 2 + self.core, self.z)
        return ((there * 4 + self.x) * 2 + self.core, self.z)

    def share(self):
        return lax.rem(self.z - self.d + 32, 4)


class Links:
    def __init__(self, send_sem, recv_sem):
        self.send_sem, self.recv_sem, self.used, self.made = send_sem, recv_sem, 0, []

    def send(self, src, dst, device):
        copy = pltpu.make_async_remote_copy(
            src_ref=src,
            dst_ref=dst,
            send_sem=self.send_sem.at[self.used],
            recv_sem=self.recv_sem.at[self.used],
            device_id=device,
            device_id_type=MESH,
        )
        self.used += 1
        copy.start()
        self.made.append(copy)
        return copy

    def drain(self):
        for copy in self.made:
            copy.wait_send()


def greet(place, near, far=False):
    barrier = pltpu.get_barrier_semaphore()
    for axis, by in near:
        pl.semaphore_signal(
            barrier, inc=1, device_id=place.device(axis, by), device_id_type=MESH
        )
    count = len(near)
    if far:
        share = place.share()
        for j in range(8):
            peer = j * 4 + share

            @pl.when(peer != place.d)
            def _():
                pl.semaphore_signal(
                    barrier, inc=1, device_id=(peer, place.z), device_id_type=MESH
                )

        mine = (lax.rem(place.d, 4) == share).astype(I32)
        pl.semaphore_wait(barrier, count + 8 - mine)
    else:
        pl.semaphore_wait(barrier, count)


def peer_copy(place, src, dst, j, send_sem, recv_sem, out):
    return pltpu.make_async_remote_copy(
        src_ref=src,
        dst_ref=dst,
        send_sem=send_sem.at[j],
        recv_sem=recv_sem.at[lax.div(place.d, 4) if out else j],
        device_id=(j * 4 + place.share(), place.z),
        device_id_type=MESH,
    )


def block_copy(src, dst, sem, block):
    return pltpu.make_async_copy(src.at[block], dst.at[block], sem.at[block])


def exchange_body(
    adj, hub_in, halo_in, deg_out, hub_out, halo_out,
    buf, deg_all, deg_mine, adj_sem, local_sem, send_sem, recv_sem, far_send, far_recv,
):
    place = Place()
    x, y, c, d, z = place.x, place.y, place.core, place.d, place.z
    share = place.share()
    blocks = adj.shape[0]
    for b in range(blocks):
        block_copy(adj, buf, adj_sem, b).start()
    own_hub = pltpu.make_async_copy(hub_in, hub_out.at[y, x, c], local_sem.at[0])
    own_hub.start()
    near = [("x", 1), ("x", -1), ("y", 1), ("y", -1), ("z", 1), ("z", -1), ("z", 2), ("core", 1)]
    greet(place, near, far=True)
    links = Links(send_sem, recv_sem)

    first = {}
    for axis, half in (("x", 0), ("y", 1)):
        for by in (1, -1):
            first[axis, by] = links.send(
                hub_in.at[half], hub_out.at[y, x, c, half], place.device(axis, by)
            )
    here = lax.div(d, 4)
    for j in range(8):

        @pl.when(j * 4 + share != d)
        def _():
            there = halo_out.at[here, lax.rem(d, 4)]
            peer_copy(place, halo_in.at[j], there, j, far_send, far_recv, True).start()

        @pl.when(j * 4 + share == d)
        def _():
            keep = pltpu.make_async_copy(halo_in.at[j], halo_out.at[j, share], local_sem.at[1])
            keep.start()
            keep.wait()

    def degrees(low, high):
        @pl.loop(low, high)
        def _(b):
            block_copy(adj, buf, adj_sem, b).wait()
            by_column = jnp.sum(buf[b].astype(F32), axis=1)
            rows = lax.dot_general(
                jnp.ones((8, by_column.shape[1]), F32),
                by_column,
                (((1,), (1,)), ((), ())),
                precision=lax.Precision.HIGHEST,
                preferred_element_type=F32,
            )
            deg_mine[pl.ds(b, 1), :] = rows[0:1]

    degrees(0, 4)
    relay = {}
    for axis, half in (("x", 0), ("y", 1)):
        for by, part in ((1, 0), (-1, 1)):
            first[axis, by].wait_recv()
            back = place.step(axis, -by)
            at = (y, back) if axis == "x" else (back, x)
            piece = hub_out.at[at[0], at[1], c, half, pl.ds(part * 128, 128)]
            relay[axis, by] = links.send(piece, piece, place.device(axis, by))
    degrees(4, blocks)
    deg_all[z] = deg_mine[...]
    deg_copies = [
        links.send(deg_mine, deg_all.at[z], place.device("z", by)) for by in (1, -1, 2)
    ]

    own_hub.wait()
    second = {}
    for axis, other, half in (("x", "y", 0), ("y", "x", 1)):
        relay[axis, 1].wait_recv()
        relay[axis, -1].wait_recv()
        line = hub_out.at[y, :, c, half] if axis == "x" else hub_out.at[:, x, c, half]
        for by in (1, -1):
            second[other, by] = links.send(line, line, place.device(other, by))
    for axis, half in (("x", 0), ("y", 1)):
        line = hub_out.at[y, :, c, half] if axis == "x" else hub_out.at[:, x, c, half]
        second["core", axis] = links.send(line, line, place.device("core", 1))

    for j in range(8):

        @pl.when(j * 4 + share != d)
        def _():
            come = peer_copy(
                place, halo_in.at[j], halo_out.at[j, share], j, far_send, far_recv, False
            )
            come.wait_recv()
            come.wait_send()

    mine = halo_out.at[:, share]
    halo_first = {by: links.send(mine, mine, place.device("z", by)) for by in (1, -1)}

    third = {}
    last = []
    for axis, other, half in (("x", "y", 0), ("y", "x", 1)):
        for by, part in ((1, 0), (-1, 1)):
            second[other, by].wait_recv()
            back = place.step(other, -by)
            if axis == "x":
                line = hub_out.at[back, :, c, half]
                piece = hub_out.at[back, pl.ds(part * 2, 2), c, half]
            else:
                line = hub_out.at[:, back, c, half]
                piece = hub_out.at[pl.ds(part * 2, 2), back, c, half]
            third[other, by] = links.send(piece, piece, place.device(other, by))
            last.append(links.send(line, line, place.device("core", 1)))

    halo_relay = []
    for by, part in ((1, 0), (-1, 1)):
        halo_first[by].wait_recv()
        back = lax.rem(place.step("z", -by) - d + 32, 4)
        piece = halo_out.at[pl.ds(part * 4, 4), back]
        halo_relay.append(links.send(piece, piece, place.device("z", by)))

    for axis, other, half in (("x", "y", 0), ("y", "x", 1)):
        third[other, 1].wait_recv()
        third[other, -1].wait_recv()
        back = place.step(other, 2)
        line = hub_out.at[back, :, c, half] if axis == "x" else hub_out.at[:, back, c, half]
        last.append(links.send(line, line, place.device("core", 1)))

    for copy in deg_copies:
        copy.wait_recv()
    deg_out[...] = (deg_all[0] + deg_all[1]) + (deg_all[2] + deg_all[3])
    for copy in halo_relay + last + [second["core", "x"], second["core", "y"]]:
        copy.wait_recv()
    links.drain()


def exchange(adj, hub_in, halo_in):
    blocks, rows, _, _ = adj.shape
    hubs, feat = hub_in.shape
    return pl.pallas_call(
        exchange_body,
        in_specs=[ANY, ANY, ANY],
        out_specs=[VMEM, ANY, ANY],
        out_shape=[
            jax.ShapeDtypeStruct((blocks, rows), F32),
            jax.ShapeDtypeStruct((4, 4, 2, 2, hubs // 2, feat), BF16),
            jax.ShapeDtypeStruct((8, 4) + halo_in.shape[1:], BF16),
        ],
        scratch_shapes=[
            pltpu.VMEM(adj.shape, BF16),
            pltpu.VMEM((4, blocks, rows), F32),
            pltpu.VMEM((blocks, rows), F32),
            DMA((blocks,)),
            DMA((2,)),
            DMA((32,)),
            DMA((32,)),
            DMA((8,)),
            DMA((8,)),
        ],
        compiler_params=remote_params(0),
    )(adj, hub_in.reshape(2, hubs // 2, feat), halo_in)


def split_slots(tiles, adj_block):
    rows = adj_block.shape[0]
    for g in range(rows // 16):
        tiles[:, pl.ds(g * 16, 16), :] = jnp.swapaxes(adj_block[pl.ds(g * 16, 16)], 0, 1)


def products_body(
    src, adj, grads, w_neigh, deg, own, hub, halo, own_out, far_out, num,
    table, rows_in, buf, tiles, sem, in_sem, out_sem,
):
    blocks, rows, slots, _ = adj.shape
    for b in range(blocks):
        block_copy(adj, buf, sem, b).start()
    copies = []
    start = 0
    for i, part in enumerate((own, hub, halo)):
        count = part.shape[0]
        copies.append(pltpu.make_async_copy(part, rows_in.at[pl.ds(start, count)], in_sem.at[i]))
        start += count
    for copy in copies:
        copy.start()

    @pl.loop(0, table.shape[0], unroll=8)
    def _(c):
        table[c] = jnp.zeros(table.shape[1:], F32)

    for copy in copies:
        copy.wait()

    @pl.loop(0, blocks)
    def _(b):
        block_copy(adj, buf, sem, b).wait()
        split_slots(tiles, buf.at[b])
        grad_t = lax.dot_general(
            w_neigh[...],
            grads[pl.ds(pl.multiple_of(b * rows, rows), rows), :],
            (((1,), (1,)), ((), ())),
            preferred_element_type=F32,
        )
        grad_t = grad_t / jnp.maximum(deg[pl.ds(b, 1), :], 1.0)
        high = grad_t.astype(BF16)
        low = (grad_t - high.astype(F32)).astype(BF16)
        both = jnp.concatenate([high, low], axis=1)
        total = jnp.zeros((rows, num.shape[1]), F32)
        for k in range(0, slots, 2):
            c0, c1 = src[b, k], src[b, k + 1]
            pair = jnp.concatenate([tiles[k], tiles[k + 1]], axis=1)
            part = jnp.dot(both, jnp.concatenate([pair, pair], axis=0), preferred_element_type=F32)
            table[c0] += part[:, : part.shape[1] // 2]
            table[c1] += part[:, part.shape[1] // 2 :]
            rhs = jnp.concatenate([rows_in[c0], rows_in[c1]], axis=0)
            total = total + jnp.dot(pair, rhs, preferred_element_type=F32)
        num[pl.ds(pl.multiple_of(b * rows, rows), rows), :] = total

    own_blocks = own.shape[0]
    far_blocks = table.shape[0] - own_blocks
    far = pltpu.make_async_copy(table.at[pl.ds(own_blocks, far_blocks)], far_out, out_sem.at[0])
    far.start()
    outs = []
    step = own_blocks // 4
    for g in range(4):

        @pl.loop(g * step, (g + 1) * step, unroll=4)
        def _(c):
            table[c] = table[c].T

        part = pl.ds(g * step, step)
        outs.append(pltpu.make_async_copy(table.at[part], own_out.at[part], out_sem.at[1 + g]))
        outs[-1].start()
    for copy in outs:
        copy.wait()
    far.wait()


def products(src, adj, grads, w_neigh, deg, own, hub, halo):
    blocks, rows, slots, cols = adj.shape
    feat = grads.shape[1]
    far_blocks = hub.shape[0] + halo.shape[0]
    table_blocks = own.shape[0] + far_blocks
    return pl.pallas_call(
        products_body,
        in_specs=[SMEM, ANY, VMEM, VMEM, VMEM, ANY, ANY, ANY],
        out_specs=[ANY, ANY, VMEM],
        out_shape=[
            jax.ShapeDtypeStruct((own.shape[0], cols, feat), F32),
            jax.ShapeDtypeStruct((far_blocks, feat, cols), F32),
            jax.ShapeDtypeStruct((blocks * rows, feat), F32),
        ],
        scratch_shapes=[
            pltpu.VMEM((table_blocks, feat, cols), F32),
            pltpu.VMEM((table_blocks, cols, feat), BF16),
            pltpu.VMEM(adj.shape, BF16),
            pltpu.VMEM((slots, rows, cols), BF16),
            DMA((blocks,)),
            DMA((3,)),
            DMA((5,)),
        ],
        compiler_params=PARAMS,
    )(src, adj, grads, w_neigh, deg, own, hub, halo)


def encode(block):
    top = jnp.maximum(jnp.max(jnp.abs(block), axis=0, keepdims=True), 1e-33)
    return jnp.round(block * (TOP / top)).astype(I32).astype(I16), top * (1.0 / TOP)


def decode(code, scale):
    return code.astype(I32).astype(F32) * scale


class Packet:
    def __init__(self, codes, scales=None):
        self.codes, self.scales = codes, scales

    def put(self, i, block):
        if self.scales is None:
            self.codes[i] = block
        else:
            self.codes[i], self.scales[i] = encode(block)

    def get(self, i):
        if self.scales is None:
            return self.codes[i]
        return decode(self.codes[i], self.scales[i])

    def send(self, links, there, device):
        copies = [links.send(self.codes, there.codes, device)]
        if self.scales is not None:
            copies.append(links.send(self.scales, there.scales, device))
        return copies


class RingSum:
    def __init__(self, place, links, axis, count, load, out_bufs, in_bufs):
        self.place, self.links, self.axis, self.count, self.load = place, links, axis, count, load
        self.out = [Packet(*[ref.at[m] for ref in out_bufs]) for m in range(6)]
        self.come = [Packet(*[ref.at[m] for ref in in_bufs]) for m in range(6)]
        self.copies = {}

    def push(self, m, by, block):
        @pl.loop(0, self.count)
        def _(i):
            self.out[m].put(i, block(i))

        self.copies[m] = self.out[m].send(
            self.links, self.come[m], self.place.device(self.axis, by)
        )

    def wait(self, m):
        for copy in self.copies[m]:
            copy.wait_recv()

    def start(self):
        opposite = self.place.step(self.axis, 2)
        for m, by, half in ((0, 1, 0), (1, -1, 1)):
            self.push(m, by, lambda i, half=half: self.load(opposite, half, i))
        for m, by, half in ((2, 1, 1), (3, -1, 0)):
            there = self.place.step(self.axis, by)
            self.push(m, by, lambda i, there=there, half=half: self.load(there, half, i))

    def relay(self):
        for m, by, half in ((4, 1, 0), (5, -1, 1)):
            there = self.place.step(self.axis, by)
            self.wait(m - 4)
            self.push(
                m,
                by,
                lambda i, there=there, half=half, m=m: self.load(there, half, i)
                + self.come[m - 4].get(i),
            )

    def finish(self, store):
        here = self.place.at(self.axis)
        for half, a, b in ((0, 4, 3), (1, 5, 2)):
            self.wait(a)
            self.wait(b)

            @pl.loop(0, self.count)
            def _(i):
                store(
                    half,
                    i,
                    self.load(here, half, i) + (self.come[a].get(i) + self.come[b].get(i)),
                )


def ring_scratch(count, coded):
    tile = (6, count, BLK, BLK)
    if not coded:
        return [pltpu.VMEM(tile, F32)] * 2
    pair = [pltpu.VMEM(tile, I16), pltpu.VMEM((6, count, 1, BLK), F32)]
    return pair + pair


def ring_bufs(refs, coded):
    n = 2 if coded else 1
    return refs[:n], refs[n:]


def owners_body(far, num_in, hub_out, halo_out, num_out, mine, theirs, lists, num, *rest):
    (core_out, core_scale_out, core_in, core_scale_in), rest = rest[:4], rest[4:]
    rings = []
    for coded in (True, True, True, True, True, False):
        n = 4 if coded else 2
        rings.append(ring_bufs(rest[:n], coded))
        rest = rest[n:]
    line_x, line_y, list_sum, list_out, list_scale_out, list_in, list_scale_in = rest[:7]
    load_sem, send_sem, recv_sem, far_send, far_recv, far_send2, far_recv2 = rest[7:]
    place = Place()
    x, y, c, d, z = place.x, place.y, place.core, place.d, place.z
    share = place.share()
    links = Links(send_sem, recv_sem)

    hub_far = far.at[pl.ds(0, 128)].reshape(16, 2, 4, BLK, BLK)
    loads = [
        pltpu.make_async_copy(far.at[pl.ds(128, 32)], lists, load_sem.at[0]),
        pltpu.make_async_copy(num_in, num, load_sem.at[1]),
    ]
    for g in range(4):
        loads.append(
            pltpu.make_async_copy(
                hub_far.at[pl.ds(g * 4, 4), 1 - c], theirs.at[pl.ds(g * 4, 4)], load_sem.at[2 + g]
            )
        )
    loads.append(pltpu.make_async_copy(hub_far.at[:, c], mine, load_sem.at[6]))
    for load in loads:
        load.start()
    near = [("x", 1), ("x", -1), ("y", 1), ("y", -1), ("z", 1), ("z", -1), ("core", 1)]
    greet(place, near, far=True)

    def ring(which, axis, count, load):
        return RingSum(place, links, axis, count, load, *rings[which])

    def list_for(there, half, i):
        return lists[(half * 4 + i) * 4 + lax.rem(there - d + 32, 4)]

    list_ring = ring(4, "z", 4, list_for)
    num_ring = ring(5, "z", 2, lambda there, half, i: num[there * 4 + half * 2 + i])
    loads[0].wait()
    list_ring.start()
    loads[1].wait()
    num_ring.start()

    core_copies = []
    for g in range(4):
        loads[2 + g].wait()

        @pl.loop(0, 16)
        def _(i):
            code, scale = encode(theirs[g * 4 + lax.div(i, 4), lax.rem(i, 4)])
            core_out[g, i] = code
            core_scale_out[g, i] = scale

        there = place.device("core", 1)
        core_copies.append(
            [
                links.send(core_out.at[g], core_in.at[g], there),
                links.send(core_scale_out.at[g], core_scale_in.at[g], there),
            ]
        )
    list_ring.relay()
    num_ring.relay()
    loads[6].wait()
    for g in range(4):
        for copy in core_copies[g]:
            copy.wait_recv()

        @pl.loop(0, 16)
        def _(i):
            mine[g * 4 + lax.div(i, 4), lax.rem(i, 4)] += decode(
                core_in[g, i], core_scale_in[g, i]
            )

    first_x = ring(0, "x", 4, lambda there, half, i: mine[i * 4 + there, half])
    first_y = ring(1, "y", 4, lambda there, half, i: mine[there * 4 + i, 2 + half])
    first_x.start()
    first_y.start()

    def keep_list(half, i, total):
        list_sum[half * 4 + i] = total

    list_ring.finish(keep_list)

    @pl.loop(0, 8)
    def _(j):
        code, scale = encode(list_sum[j])
        list_out[j] = code
        list_scale_out[j] = scale

    here = lax.div(d, 4)

    def list_copies(j, out):
        to = here if out else j
        return (
            peer_copy(place, list_out.at[j], list_in.at[to], j, far_send, far_recv, out),
            peer_copy(
                place, list_scale_out.at[j], list_scale_in.at[to], j, far_send2, far_recv2, out
            ),
        )

    for j in range(8):

        @pl.when(j * 4 + share != d)
        def _():
            for copy in list_copies(j, True):
                copy.start()

        @pl.when(j * 4 + share == d)
        def _():
            list_in[j] = list_out[j]
            list_scale_in[j] = list_scale_out[j]

    first_x.relay()
    first_y.relay()

    def keep_num(half, i, total):
        num_out[half * 2 + i] = total

    num_ring.finish(keep_num)

    def keep_x(half, i, total):
        line_x[i, half] = total

    def keep_y(half, i, total):
        line_y[i, half] = total

    first_x.finish(keep_x)
    first_y.finish(keep_y)
    second_x = ring(2, "y", 1, lambda there, half, i: line_x[there, half])
    second_y = ring(3, "x", 1, lambda there, half, i: line_y[there, half])
    second_x.start()
    second_y.start()

    for j in range(8):

        @pl.when(j * 4 + share != d)
        def _():
            for copy in list_copies(j, False):
                copy.wait_recv()
                copy.wait_send()

        halo_out[j] = decode(list_in[j], list_scale_in[j]).T

    second_x.relay()
    second_y.relay()

    def keep_first(half, i, total):
        hub_out[half] = total.T

    def keep_second(half, i, total):
        hub_out[2 + half] = total.T

    second_x.finish(keep_first)
    second_y.finish(keep_second)
    links.drain()


def owners(far, num):
    tile = (BLK, BLK)
    one = (1, BLK)
    return pl.pallas_call(
        owners_body,
        in_specs=[ANY, ANY],
        out_specs=[VMEM, VMEM, VMEM],
        out_shape=[
            jax.ShapeDtypeStruct((4,) + tile, F32),
            jax.ShapeDtypeStruct((8,) + tile, F32),
            jax.ShapeDtypeStruct((4,) + tile, F32),
        ],
        scratch_shapes=[
            pltpu.VMEM((16, 4) + tile, F32),
            pltpu.VMEM((16, 4) + tile, F32),
            pltpu.VMEM((32,) + tile, F32),
            pltpu.VMEM((16,) + tile, F32),
            pltpu.VMEM((4, 16) + tile, I16),
            pltpu.VMEM((4, 16) + one, F32),
            pltpu.VMEM((4, 16) + tile, I16),
            pltpu.VMEM((4, 16) + one, F32),
            *ring_scratch(4, True),
            *ring_scratch(4, True),
            *ring_scratch(1, True),
            *ring_scratch(1, True),
            *ring_scratch(4, True),
            *ring_scratch(2, False),
            pltpu.VMEM((4, 2) + tile, F32),
            pltpu.VMEM((4, 2) + tile, F32),
            pltpu.VMEM((8,) + tile, F32),
            pltpu.VMEM((8,) + tile, I16),
            pltpu.VMEM((8,) + one, F32),
            pltpu.VMEM((8,) + tile, I16),
            pltpu.VMEM((8,) + one, F32),
            DMA((7,)),
            DMA((80,)),
            DMA((80,)),
            DMA((8,)),
            DMA((8,)),
            DMA((8,)),
            DMA((8,)),
        ],
        compiler_params=remote_params(1),
    )(far, num.reshape(-1, BLK, BLK))


def settle_body(
    idx, live, where, own, hub, halo, num, deg, feats, grads, w_self, w_neigh, bias,
    own_out, layer, weights, table, self_rows, sem,
):
    share = lax.axis_index("esplit")
    step = own.shape[0] // 4
    loads = []
    for g in range(4):
        part = pl.ds(g * step, step)
        loads.append(pltpu.make_async_copy(own.at[part], table.at[part], sem.at[g]))
    first = pl.multiple_of(where[0], 128)
    loads.append(pltpu.make_async_copy(feats.at[pl.ds(first, 512)], self_rows, sem.at[4]))
    for load in loads:
        load.start()

    at = pl.multiple_of(share * 512, 512)
    my_grads = grads[pl.ds(at, 512), :]
    wide = my_grads.astype(F32)
    loads[4].wait()
    mine = self_rows[...]
    contract = (((0,), (0,)), ((), ()))
    weights[0:128, :] = lax.dot_general(mine, my_grads, contract, preferred_element_type=F32)
    neigh = jnp.zeros((128, 128), F32)
    for i in range(4):
        divisor = jnp.maximum(deg[pl.ds(share * 4 + i, 1), :], 1.0)
        aggregate = num[i] / jnp.broadcast_to(divisor, (128, 128)).T
        rows = slice(i * 128, (i + 1) * 128)
        layer[rows, :] = (
            jnp.dot(
                aggregate,
                w_neigh[...].astype(F32),
                precision=lax.Precision.HIGHEST,
                preferred_element_type=F32,
            )
            + jnp.dot(mine[rows], w_self[...], preferred_element_type=F32)
            + bias[...].astype(F32)
        ).astype(BF16)
        neigh = neigh + lax.dot_general(
            aggregate, wide[rows], contract,
            precision=lax.Precision.HIGHEST, preferred_element_type=F32,
        )
    weights[128:256, :] = neigh
    weights[256:264, :] = jnp.broadcast_to(jnp.sum(wide, axis=0, keepdims=True), (8, 128))
    for j in range(8):
        row = lax.broadcasted_iota(I32, (128, 128), 0)
        halo[pl.ds(j * 128, 128), :] = jnp.where(
            row < live[j], halo[pl.ds(j * 128, 128), :], 0.0
        )
    back = lax.dot_general(
        my_grads, w_self[...], (((1,), (1,)), ((), ())), preferred_element_type=F32
    )
    for load in loads[:4]:
        load.wait()
    table[pl.ds(first, 512), :] += back

    def scatter(rows, base, count):
        @pl.loop(0, count // 8)
        def _(g):
            places = [idx[base + g * 8 + i] for i in range(8)]
            values = [
                table[pl.ds(places[i], 1), :] + rows[pl.ds(g * 8 + i, 1), :] for i in range(8)
            ]
            for i in range(8):
                table[pl.ds(places[i], 1), :] = values[i]

    scatter(hub, 0, 512)
    for j in range(8):
        scatter(halo.at[pl.ds(j * 128, 128)], 512 + j * 128, 128)
    outs = []
    for g in range(4):
        part = pl.ds(g * step, step)
        outs.append(pltpu.make_async_copy(table.at[part], own_out.at[part], sem.at[g]))
        outs[-1].start()
    for out in outs:
        out.wait()


def settle(idx, live, where, own, hub, halo, num, deg, feats, grads, w_self, w_neigh, bias):
    return pl.pallas_call(
        settle_body,
        in_specs=[SMEM, SMEM, SMEM, ANY, VMEM, VMEM, VMEM, VMEM, ANY, VMEM, VMEM, VMEM, VMEM],
        out_specs=[ANY, VMEM, VMEM],
        out_shape=[
            jax.ShapeDtypeStruct(own.shape, F32),
            jax.ShapeDtypeStruct((512, 128), BF16),
            jax.ShapeDtypeStruct((264, 128), F32),
        ],
        scratch_shapes=[pltpu.VMEM(own.shape, F32), pltpu.VMEM((512, 128), BF16), DMA((5,))],
        compiler_params=PARAMS,
    )(idx, live, where, own, hub, halo, num, deg, feats, grads, w_self, w_neigh, bias)


def final_body(own, weights, out, weights_out, table, *rest):
    rings = []
    for _ in range(4):
        rings.append(ring_bufs(rest[:4], True))
        rest = rest[4:]
    sums, slots, load_sem, out_sem, send_sem, recv_sem = rest
    place = Place()
    links = Links(send_sem, recv_sem)
    z = place.z
    loads = []
    for i, by in enumerate((2, 1, -1, 0)):
        part = pl.ds(place.step("z", by) * 32, 32)
        loads.append(pltpu.make_async_copy(own.at[part], table.at[part], load_sem.at[i]))
        loads[-1].start()
    near = [(axis, by) for axis in ("x", "y", "z") for by in (1, -1, 2)] + [("core", 1)]
    greet(place, near)

    def load(g):
        return lambda there, half, i: table[there * 32 + half * 16 + g * 4 + i]

    flows = [RingSum(place, links, "z", 4, load(g), *rings[g]) for g in range(4)]
    for stage in range(3):
        loads[stage].wait()
    for flow in flows:
        flow.start()

    def all_sum(stage, axis):
        mine = place.core if axis == "core" else place.at(axis)
        there = [1] if axis == "core" else [1, -1, 2]
        copies = [
            links.send(sums.at[stage], slots.at[stage, mine], place.device(axis, by))
            for by in there
        ]
        slots[stage, mine] = sums[stage]

        def end():
            for copy in copies:
                copy.wait_recv()
            total = slots[stage, 0] + slots[stage, 1]
            if axis != "core":
                total = total + (slots[stage, 2] + slots[stage, 3])
            if stage == 3:
                weights_out[...] = total
            else:
                sums[stage + 1] = total

        return end

    sums[0] = weights[...]
    end = all_sum(0, "core")
    flows[0].relay()
    end()
    end = all_sum(1, "x")
    flows[1].relay()
    flows[2].relay()
    end()
    end = all_sum(2, "y")
    flows[3].relay()
    end()
    end = all_sum(3, "z")
    loads[3].wait()
    outs = []
    for g in range(4):

        def store(half, i, total, g=g):
            table[z * 32 + half * 16 + g * 4 + i] = total

        flows[g].finish(store)
        for half in range(2):
            outs.append(
                pltpu.make_async_copy(
                    table.at[pl.ds(z * 32 + half * 16 + g * 4, 4)],
                    out.at[pl.ds(half * 16 + g * 4, 4)],
                    out_sem.at[g * 2 + half],
                )
            )
            outs[-1].start()
    end()
    for copy in outs:
        copy.wait()
    links.drain()


def final(own, weights):
    tile = (BLK, BLK)
    scratch = []
    for _ in range(4):
        scratch += ring_scratch(4, True)
    return pl.pallas_call(
        final_body,
        in_specs=[ANY, VMEM],
        out_specs=[ANY, VMEM],
        out_shape=[
            jax.ShapeDtypeStruct((32,) + tile, F32),
            jax.ShapeDtypeStruct(weights.shape, F32),
        ],
        scratch_shapes=[
            pltpu.VMEM((128,) + tile, F32),
            *scratch,
            pltpu.VMEM((4,) + weights.shape, F32),
            pltpu.VMEM((4, 4) + weights.shape, F32),
            DMA((4,)),
            DMA((8,)),
            DMA((64,)),
            DMA((64,)),
        ],
        compiler_params=remote_params(2),
    )(own, weights)


def local(
    features,
    adjacency,
    tile_source,
    hub_rows,
    send_rows,
    send_live,
    target_block,
    w_self,
    w_neigh,
    out_bias,
    out_grad,
):
    own_count, feat = features.shape
    peers = lax.axis_size("dom")
    d = lax.axis_index("dom")
    z = lax.axis_index("esplit")
    adj = adjacency[0, 0]
    src = tile_source[0, 0]
    blocks, rows, _, cols = adj.shape
    targets = blocks * rows
    hub_idx = hub_rows[0]
    hubs = hub_idx.shape[0]
    share = lax.rem(z - d + peers, 4)
    slots = send_rows.shape[2]
    lists = lax.dynamic_index_in_dim(send_rows[0].reshape(8, 4, slots), share, 1, keepdims=False)
    live = lax.dynamic_index_in_dim(send_live[0].reshape(8, 4), share, 1, keepdims=False)
    idx = jnp.concatenate([hub_idx, lists.reshape(-1)])
    picked = features[idx]
    hub_local = picked[:hubs]
    alive = jnp.arange(slots, dtype=I32)[None, :] < live[:, None]
    halo_local = jnp.where(
        alive[:, :, None], picked[hubs:].reshape(8, slots, feat), jnp.zeros((), features.dtype)
    )
    deg, hub_all, halo_all = exchange(adj, hub_local, halo_local)
    own, far, num = products(
        src,
        adj,
        out_grad,
        w_neigh,
        deg,
        features.reshape(-1, cols, feat),
        hub_all.reshape(-1, cols, feat),
        halo_all.reshape(-1, cols, feat),
    )
    hub_grad, halo_grad, num_sum = owners(far, num)
    where = target_block * rows + z * (targets // 4)
    own, layer, weights = settle(
        idx,
        live,
        where,
        own.reshape(-1, feat),
        hub_grad.reshape(-1, feat),
        halo_grad.reshape(-1, feat),
        num_sum,
        deg,
        features,
        out_grad,
        w_self,
        w_neigh,
        out_bias[None, :],
    )
    grad_features, weights = final(own.reshape(-1, BLK, feat), weights)
    weights = weights / math.sqrt(targets * peers)
    return (
        layer,
        grad_features.reshape(-1, feat),
        weights[:feat],
        weights[feat : 2 * feat],
        weights[2 * feat],
    )


def solution(mesh):
    in_specs = (
        P("dom", None),
        P("dom", "esplit", None, None, None, None),
        P("dom", "esplit", None, None),
        P("dom", None),
        P("dom", None, None),
        P("dom", None),
        P("dom"),
        P(),
        P(),
        P(),
        P("dom", None),
    )
    out_specs = (P(("dom", "esplit"), None), P(("dom", "esplit"), None), P(), P(), P())
    return jax.shard_map(local, mesh=mesh, in_specs=in_specs, out_specs=out_specs, check_vma=False)
```

```python
import math

import jax
import jax.numpy as jnp
from jax import lax
from jax.experimental import pallas as pl
from jax.experimental.pallas import tpu as pltpu
from jax.sharding import PartitionSpec as P

F32 = jnp.float32
BF16 = jnp.bfloat16
I16 = jnp.int16
I32 = jnp.int32
MESH = pl.DeviceIdType.MESH
DMA = pltpu.SemaphoreType.DMA
VMEM_LIMIT = 56 * 2**20
ANY = pl.BlockSpec(memory_space=pl.ANY)
SMEM = pl.BlockSpec(memory_space=pltpu.SMEM)
VMEM = pl.BlockSpec(memory_space=pltpu.VMEM)
PARAMS = pltpu.CompilerParams(vmem_limit_bytes=VMEM_LIMIT)
BLK = 128
TOP = 32767.0


def remote_params(number):
    return pltpu.CompilerParams(
        vmem_limit_bytes=VMEM_LIMIT, collective_id=number, has_side_effects=True
    )


class Place:
    def __init__(self):
        self.d = lax.axis_index("dom")
        self.z = lax.axis_index("esplit")
        self.core = lax.rem(self.d, 2)
        self.x = lax.rem(lax.div(self.d, 2), 4)
        self.y = lax.div(self.d, 8)

    def at(self, axis):
        return {"x": self.x, "y": self.y, "z": self.z}[axis]

    def step(self, axis, by):
        return lax.rem(self.at(axis) + (by + 4), 4)

    def device(self, axis, by):
        if axis == "core":
            return (self.d + 1 - 2 * self.core, self.z)
        there = self.step(axis, by)
        if axis == "z":
            return (self.d, there)
        if axis == "x":
            return ((self.y * 4 + there) * 2 + self.core, self.z)
        return ((there * 4 + self.x) * 2 + self.core, self.z)

    def share(self):
        return lax.rem(self.z - self.d + 32, 4)


class Links:
    def __init__(self, send_sem, recv_sem):
        self.send_sem, self.recv_sem, self.used, self.made = send_sem, recv_sem, 0, []

    def send(self, src, dst, device):
        assert self.used < self.send_sem.shape[0]
        copy = pltpu.make_async_remote_copy(
            src_ref=src,
            dst_ref=dst,
            send_sem=self.send_sem.at[self.used],
            recv_sem=self.recv_sem.at[self.used],
            device_id=device,
            device_id_type=MESH,
        )
        self.used += 1
        copy.start()
        self.made.append(copy)
        return copy

    def drain(self):
        for copy in self.made:
            copy.wait_send()


def greet(place, near, far=False):
    barrier = pltpu.get_barrier_semaphore()
    for axis, by in near:
        pl.semaphore_signal(
            barrier, inc=1, device_id=place.device(axis, by), device_id_type=MESH
        )
    count = len(near)
    if far:
        share = place.share()
        for j in range(8):
            peer = j * 4 + share

            @pl.when(peer != place.d)
            def _():
                pl.semaphore_signal(
                    barrier, inc=1, device_id=(peer, place.z), device_id_type=MESH
                )

        count = count + 8 - (lax.rem(place.d, 4) == share).astype(I32)

    def wait():
        pl.semaphore_wait(barrier, count)

    return wait


def peer_copy(place, src, dst, j, send_sem, recv_sem, out):
    return pltpu.make_async_remote_copy(
        src_ref=src,
        dst_ref=dst,
        send_sem=send_sem.at[j],
        recv_sem=recv_sem.at[lax.div(place.d, 4) if out else j],
        device_id=(j * 4 + place.share(), place.z),
        device_id_type=MESH,
    )


def block_copy(src, dst, sem, block):
    return pltpu.make_async_copy(src.at[block], dst.at[block], sem.at[block])


def exchange_body(
    adj, hub_in, halo_in, deg_out, hub_out, halo_out,
    buf, deg_all, deg_mine, adj_sem, local_sem, send_sem, recv_sem, far_send, far_recv,
):
    place = Place()
    x, y, c, d, z = place.x, place.y, place.core, place.d, place.z
    share = place.share()
    blocks = adj.shape[0]
    near = [("x", 1), ("x", -1), ("y", 1), ("y", -1), ("z", 1), ("z", -1), ("z", 2), ("core", 1)]
    ready = greet(place, near, far=True)
    for b in range(blocks):
        block_copy(adj, buf, adj_sem, b).start()
    own_hub = pltpu.make_async_copy(hub_in, hub_out.at[y, x, c], local_sem.at[0])
    own_hub.start()
    links = Links(send_sem, recv_sem)

    def degrees(low, high):
        @pl.loop(low, high)
        def _(b):
            block_copy(adj, buf, adj_sem, b).wait()
            by_column = jnp.sum(buf[b].astype(F32), axis=1)
            rows = lax.dot_general(
                jnp.ones((8, by_column.shape[1]), F32),
                by_column,
                (((1,), (1,)), ((), ())),
                precision=lax.Precision.HIGHEST,
                preferred_element_type=F32,
            )
            deg_mine[pl.ds(b, 1), :] = rows[0:1]

    flows = (("x", "y", 0), ("y", "x", 1))
    cores = []

    def piece(flow, along, across, rows=None):
        axis, other, half = flow
        p, q = place.step(axis, along), place.step(other, across)
        at = (q, p) if axis == "x" else (p, q)
        if rows is None:
            return hub_out.at[at[0], at[1], c, half]
        return hub_out.at[at[0], at[1], c, half, pl.ds(rows * 128, 128)]

    def pass_on(ref, axis, by):
        return links.send(ref, ref, place.device(axis, by))

    def to_core(ref):
        cores.append(pass_on(ref, "core", 1))

    first, relay, second, third = {}, {}, {}, {}
    degrees(0, 1)
    ready()
    for flow in flows:
        axis, other, half = flow
        for by in (1, -1):
            first[axis, by] = links.send(
                hub_in.at[half], piece(flow, 0, 0), place.device(axis, by)
            )
    here = lax.div(d, 4)
    for j in range(8):

        @pl.when(j * 4 + share != d)
        def _():
            there = halo_out.at[here, lax.rem(d, 4)]
            peer_copy(place, halo_in.at[j], there, j, far_send, far_recv, True).start()

        @pl.when(j * 4 + share == d)
        def _():
            keep = pltpu.make_async_copy(halo_in.at[j], halo_out.at[j, share], local_sem.at[1])
            keep.start()
            keep.wait()

    for flow in flows:
        axis, other, half = flow
        for by in (1, -1):
            second[axis, 0, by] = links.send(
                hub_in.at[half], piece(flow, 0, 0), place.device(other, by)
            )
    degrees(1, 4)
    own_hub.wait()
    for flow in flows:
        to_core(piece(flow, 0, 0))
        axis, other, half = flow
        for by, part in ((1, 0), (-1, 1)):
            first[axis, by].wait_recv()
            relay[axis, by] = pass_on(piece(flow, -by, 0, part), axis, by)
        for along in (-1, 1):
            for by in (1, -1):
                second[axis, along, by] = pass_on(piece(flow, along, 0), other, by)
            to_core(piece(flow, along, 0))

    def carry(flow, along):
        axis, other, half = flow
        forward = 1 if along in (0, 2) else -1
        for by in (1, -1):
            second[axis, along, by].wait_recv()
            if by == forward:
                third[axis, along] = pass_on(piece(flow, along, -by), other, by)
            to_core(piece(flow, along, -by))

    degrees(4, 7)
    for flow in flows:
        carry(flow, 0)
    halo_first, halo_relay = {}, []
    for j in range(8):

        @pl.when(j * 4 + share != d)
        def _():
            come = peer_copy(
                place, halo_in.at[j], halo_out.at[j, share], j, far_send, far_recv, False
            )
            come.wait_recv()
            come.wait_send()

        for by in (1, -1):
            halo_first[j, by] = pass_on(halo_out.at[j, share], "z", by)
    for flow in flows:
        axis, other, half = flow
        relay[axis, 1].wait_recv()
        relay[axis, -1].wait_recv()
        for by in (1, -1):
            second[axis, 2, by] = pass_on(piece(flow, 2, 0), other, by)
        to_core(piece(flow, 2, 0))
    degrees(7, blocks)
    deg_all[z] = deg_mine[...]
    deg_copies = [
        links.send(deg_mine, deg_all.at[z], place.device("z", by)) for by in (1, -1, 2)
    ]
    for along in (-1, 1):
        for flow in flows:
            carry(flow, along)
    for j in range(8):
        for by in (1, -1):
            halo_first[j, by].wait_recv()
            if (by == 1) == (j % 2 == 0):
                back = lax.rem(place.step("z", -by) - d + 32, 4)
                halo_relay.append(pass_on(halo_out.at[j, back], "z", by))
    for flow in flows:
        carry(flow, 2)
    for along in (0, -1, 1, 2):
        for flow in flows:
            third[flow[0], along].wait_recv()
            to_core(piece(flow, along, 2))
    for copy in deg_copies:
        copy.wait_recv()
    deg_out[...] = (deg_all[0] + deg_all[1]) + (deg_all[2] + deg_all[3])
    for copy in halo_relay + cores:
        copy.wait_recv()
    links.drain()


def exchange(adj, hub_in, halo_in):
    blocks, rows, _, _ = adj.shape
    hubs, feat = hub_in.shape
    return pl.pallas_call(
        exchange_body,
        in_specs=[ANY, ANY, ANY],
        out_specs=[VMEM, ANY, ANY],
        out_shape=[
            jax.ShapeDtypeStruct((blocks, rows), F32),
            jax.ShapeDtypeStruct((4, 4, 2, 2, hubs // 2, feat), BF16),
            jax.ShapeDtypeStruct((8, 4) + halo_in.shape[1:], BF16),
        ],
        scratch_shapes=[
            pltpu.VMEM(adj.shape, BF16),
            pltpu.VMEM((4, blocks, rows), F32),
            pltpu.VMEM((blocks, rows), F32),
            DMA((blocks,)),
            DMA((2,)),
            DMA((96,)),
            DMA((96,)),
            DMA((8,)),
            DMA((8,)),
        ],
        compiler_params=remote_params(0),
    )(adj, hub_in.reshape(2, hubs // 2, feat), halo_in)


def split_slots(tiles, adj_block):
    rows = adj_block.shape[0]
    for g in range(rows // 16):
        tiles[:, pl.ds(g * 16, 16), :] = jnp.swapaxes(adj_block[pl.ds(g * 16, 16)], 0, 1)


def products_body(
    src, adj, grads, w_neigh, deg, own, hub, halo, own_out, far_out, num,
    table, rows_in, buf, tiles, sem, in_sem, out_sem,
):
    blocks, rows, slots, _ = adj.shape
    for b in range(blocks):
        block_copy(adj, buf, sem, b).start()
    copies = []
    start = 0
    for i, part in enumerate((own, hub, halo)):
        count = part.shape[0]
        copies.append(pltpu.make_async_copy(part, rows_in.at[pl.ds(start, count)], in_sem.at[i]))
        start += count
    for copy in copies:
        copy.start()

    @pl.loop(0, table.shape[0], unroll=8)
    def _(c):
        table[c] = jnp.zeros(table.shape[1:], F32)

    for copy in copies:
        copy.wait()

    @pl.loop(0, blocks)
    def _(b):
        block_copy(adj, buf, sem, b).wait()
        split_slots(tiles, buf.at[b])
        grad_t = lax.dot_general(
            w_neigh[...],
            grads[pl.ds(pl.multiple_of(b * rows, rows), rows), :],
            (((1,), (1,)), ((), ())),
            preferred_element_type=F32,
        )
        grad_t = grad_t / jnp.maximum(deg[pl.ds(b, 1), :], 1.0)
        high = grad_t.astype(BF16)
        low = (grad_t - high.astype(F32)).astype(BF16)
        both = jnp.concatenate([high, low], axis=1)
        total = jnp.zeros((rows, num.shape[1]), F32)
        for k in range(0, slots, 2):
            c0, c1 = src[b, k], src[b, k + 1]
            pair = jnp.concatenate([tiles[k], tiles[k + 1]], axis=1)
            part = jnp.dot(both, jnp.concatenate([pair, pair], axis=0), preferred_element_type=F32)
            table[c0] += part[:, : part.shape[1] // 2]
            table[c1] += part[:, part.shape[1] // 2 :]
            rhs = jnp.concatenate([rows_in[c0], rows_in[c1]], axis=0)
            total = total + jnp.dot(pair, rhs, preferred_element_type=F32)
        num[pl.ds(pl.multiple_of(b * rows, rows), rows), :] = total

    own_blocks = own.shape[0]
    far_blocks = table.shape[0] - own_blocks
    far = pltpu.make_async_copy(table.at[pl.ds(own_blocks, far_blocks)], far_out, out_sem.at[0])
    far.start()
    outs = []
    step = own_blocks // 4
    for g in range(4):

        @pl.loop(g * step, (g + 1) * step, unroll=4)
        def _(c):
            table[c] = table[c].T

        part = pl.ds(g * step, step)
        outs.append(pltpu.make_async_copy(table.at[part], own_out.at[part], out_sem.at[1 + g]))
        outs[-1].start()
    for copy in outs:
        copy.wait()
    far.wait()


def products(src, adj, grads, w_neigh, deg, own, hub, halo):
    blocks, rows, slots, cols = adj.shape
    feat = grads.shape[1]
    far_blocks = hub.shape[0] + halo.shape[0]
    table_blocks = own.shape[0] + far_blocks
    return pl.pallas_call(
        products_body,
        in_specs=[SMEM, ANY, VMEM, VMEM, VMEM, ANY, ANY, ANY],
        out_specs=[ANY, ANY, VMEM],
        out_shape=[
            jax.ShapeDtypeStruct((own.shape[0], cols, feat), F32),
            jax.ShapeDtypeStruct((far_blocks, feat, cols), F32),
            jax.ShapeDtypeStruct((blocks * rows, feat), F32),
        ],
        scratch_shapes=[
            pltpu.VMEM((table_blocks, feat, cols), F32),
            pltpu.VMEM((table_blocks, cols, feat), BF16),
            pltpu.VMEM(adj.shape, BF16),
            pltpu.VMEM((slots, rows, cols), BF16),
            DMA((blocks,)),
            DMA((3,)),
            DMA((5,)),
        ],
        compiler_params=PARAMS,
    )(src, adj, grads, w_neigh, deg, own, hub, halo)


def encode(block):
    top = jnp.maximum(jnp.max(jnp.abs(block), axis=0, keepdims=True), 1e-33)
    return jnp.round(block * (TOP / top)).astype(I32).astype(I16), top * (1.0 / TOP)


def decode(code, scale):
    return code.astype(I32).astype(F32) * scale


class Packet:
    def __init__(self, codes, scales=None):
        self.codes, self.scales = codes, scales

    def put(self, i, block):
        if self.scales is None:
            self.codes[i] = block
        else:
            self.codes[i], self.scales[i] = encode(block)

    def get(self, i):
        if self.scales is None:
            return self.codes[i]
        return decode(self.codes[i], self.scales[i])

    def send(self, links, there, device):
        copies = [links.send(self.codes, there.codes, device)]
        if self.scales is not None:
            copies.append(links.send(self.scales, there.scales, device))
        return copies


class RingSum:
    def __init__(self, place, links, axis, count, load, out_bufs, in_bufs):
        self.place, self.links, self.axis, self.count, self.load = place, links, axis, count, load
        self.out = [Packet(*[ref.at[m] for ref in out_bufs]) for m in range(6)]
        self.come = [Packet(*[ref.at[m] for ref in in_bufs]) for m in range(6)]
        self.copies = {}

    def push(self, m, by, block):
        @pl.loop(0, self.count, unroll=min(2, self.count))
        def _(i):
            self.out[m].put(i, block(i))

        self.copies[m] = self.out[m].send(
            self.links, self.come[m], self.place.device(self.axis, by)
        )

    def wait(self, m):
        for copy in self.copies[m]:
            copy.wait_recv()

    def start_opposite(self):
        there = self.place.step(self.axis, 2)
        for m, by, half in ((0, 1, 0), (1, -1, 1)):
            self.push(m, by, lambda i, half=half: self.load(there, half, i))

    def start_near(self, by):
        m, half = (2, 1) if by == 1 else (3, 0)
        there = self.place.step(self.axis, by)
        self.push(m, by, lambda i: self.load(there, half, i))

    def start(self):
        self.start_opposite()
        self.start_near(1)
        self.start_near(-1)

    def relay(self):
        for m, by, half in ((4, 1, 0), (5, -1, 1)):
            there = self.place.step(self.axis, by)
            self.wait(m - 4)
            self.push(
                m,
                by,
                lambda i, there=there, half=half, m=m: self.load(there, half, i)
                + self.come[m - 4].get(i),
            )

    def finish(self, store):
        here = self.place.at(self.axis)
        for half, a, b in ((0, 4, 3), (1, 5, 2)):
            self.wait(a)
            self.wait(b)

            @pl.loop(0, self.count, unroll=min(2, self.count))
            def _(i):
                store(
                    half,
                    i,
                    self.load(here, half, i) + (self.come[a].get(i) + self.come[b].get(i)),
                )


def ring_scratch(count, coded):
    tile = (6, count, BLK, BLK)
    if not coded:
        return [pltpu.VMEM(tile, F32)] * 2
    pair = [pltpu.VMEM(tile, I16), pltpu.VMEM((6, count, 1, BLK), F32)]
    return pair + pair


def ring_bufs(refs, coded):
    n = 2 if coded else 1
    return refs[:n], refs[n:]


def owners_body(far, num_in, hub_out, halo_out, num_out, mine, theirs, lists, num, *rest):
    (core_out, core_scale_out, core_in, core_scale_in), rest = rest[:4], rest[4:]
    rings = []
    for coded in (True, True, True, True, True, False):
        n = 4 if coded else 2
        rings.append(ring_bufs(rest[:n], coded))
        rest = rest[n:]
    line_x, line_y, list_sum, list_out, list_scale_out, list_in, list_scale_in = rest[:7]
    load_sem, send_sem, recv_sem, far_send, far_recv, far_send2, far_recv2 = rest[7:]
    place = Place()
    x, y, c, d, z = place.x, place.y, place.core, place.d, place.z
    share = place.share()
    links = Links(send_sem, recv_sem)

    near = [("x", 1), ("x", -1), ("y", 1), ("y", -1), ("z", 1), ("z", -1), ("core", 1)]
    ready = greet(place, near, far=True)
    hub_far = far.at[pl.ds(0, 128)].reshape(4, 4, 2, 4, BLK, BLK)

    def part_of(g):
        by = (2, 1, -1, 0)[g // 2]
        if g % 2 == 0:
            return slice(None), place.step("x", by), pl.ds(0, 2)
        return place.step("y", by), slice(None), pl.ds(2, 2)

    def block_at(g, i):
        by = (2, 1, -1, 0)[g // 2]
        if g % 2 == 0:
            return lax.div(i, 2), place.step("x", by), lax.rem(i, 2)
        return place.step("y", by), lax.div(i, 2), 2 + lax.rem(i, 2)

    loads = []

    def load(src, dst):
        loads.append(pltpu.make_async_copy(src, dst, load_sem.at[len(loads)]))
        loads[-1].start()

    for g in range(8):
        p, q, t = part_of(g)
        load(hub_far.at[p, q, 1 - c, t], theirs.at[p, q, t])
    load(far.at[pl.ds(128, 32)], lists)
    load(hub_far.at[:, :, c], mine)
    load(num_in, num)

    def ring(which, axis, count, load):
        return RingSum(place, links, axis, count, load, *rings[which])

    def list_for(there, half, i):
        return lists[(half * 4 + i) * 4 + lax.rem(there - d + 32, 4)]

    list_ring = ring(4, "z", 4, list_for)
    num_ring = ring(5, "z", 2, lambda there, half, i: num[there * 4 + half * 2 + i])
    first_x = ring(0, "x", 4, lambda there, half, i: mine[i, there, half])
    first_y = ring(1, "y", 4, lambda there, half, i: mine[there, i, 2 + half])
    core_copies = []
    there = place.device("core", 1)
    for g in range(8):
        loads[g].wait()

        @pl.loop(0, 8, unroll=2)
        def _(i):
            code, scale = encode(theirs[block_at(g, i)])
            core_out[g, i] = code
            core_scale_out[g, i] = scale

        if g == 0:
            ready()
        core_copies.append(
            [
                links.send(core_out.at[g], core_in.at[g], there),
                links.send(core_scale_out.at[g], core_scale_in.at[g], there),
            ]
        )
        if g == 1:
            loads[8].wait()
            list_ring.start()

    loads[9].wait()

    def merge(g):
        for copy in core_copies[g]:
            copy.wait_recv()

        @pl.loop(0, 8, unroll=2)
        def _(i):
            at = block_at(g, i)
            mine[at] = mine[at] + decode(core_in[g, i], core_scale_in[g, i])

    merge(0)
    first_x.start_opposite()
    merge(1)
    first_y.start_opposite()
    merge(2)
    first_x.start_near(1)
    merge(3)
    first_y.start_near(1)
    merge(4)
    first_x.start_near(-1)
    merge(5)
    first_y.start_near(-1)
    list_ring.relay()
    first_x.relay()
    first_y.relay()
    loads[10].wait()
    num_ring.start()
    merge(6)
    merge(7)

    def keep_list(half, i, total):
        list_sum[half * 4 + i] = total

    list_ring.finish(keep_list)

    @pl.loop(0, 8)
    def _(j):
        code, scale = encode(list_sum[j])
        list_out[j] = code
        list_scale_out[j] = scale

    here = lax.div(d, 4)

    def list_copies(j, out):
        to = here if out else j
        return (
            peer_copy(place, list_out.at[j], list_in.at[to], j, far_send, far_recv, out),
            peer_copy(
                place, list_scale_out.at[j], list_scale_in.at[to], j, far_send2, far_recv2, out
            ),
        )

    for j in range(8):

        @pl.when(j * 4 + share != d)
        def _():
            for copy in list_copies(j, True):
                copy.start()

        @pl.when(j * 4 + share == d)
        def _():
            list_in[j] = list_out[j]
            list_scale_in[j] = list_scale_out[j]

    num_ring.relay()

    def keep_x(half, i, total):
        line_x[i, half] = total

    def keep_y(half, i, total):
        line_y[i, half] = total

    first_x.finish(keep_x)
    first_y.finish(keep_y)
    second_x = ring(2, "y", 1, lambda there, half, i: line_x[there, half])
    second_y = ring(3, "x", 1, lambda there, half, i: line_y[there, half])
    second_x.start()
    second_y.start()

    for j in range(8):

        @pl.when(j * 4 + share != d)
        def _():
            for copy in list_copies(j, False):
                copy.wait_recv()
                copy.wait_send()

        halo_out[j] = decode(list_in[j], list_scale_in[j]).T

    second_x.relay()
    second_y.relay()

    def keep_num(half, i, total):
        num_out[half * 2 + i] = total

    num_ring.finish(keep_num)

    def keep_first(half, i, total):
        hub_out[half] = total.T

    def keep_second(half, i, total):
        hub_out[2 + half] = total.T

    second_x.finish(keep_first)
    second_y.finish(keep_second)
    links.drain()


def owners(far, num):
    tile = (BLK, BLK)
    one = (1, BLK)
    return pl.pallas_call(
        owners_body,
        in_specs=[ANY, ANY],
        out_specs=[VMEM, VMEM, VMEM],
        out_shape=[
            jax.ShapeDtypeStruct((4,) + tile, F32),
            jax.ShapeDtypeStruct((8,) + tile, F32),
            jax.ShapeDtypeStruct((4,) + tile, F32),
        ],
        scratch_shapes=[
            pltpu.VMEM((4, 4, 4) + tile, F32),
            pltpu.VMEM((4, 4, 4) + tile, F32),
            pltpu.VMEM((32,) + tile, F32),
            pltpu.VMEM((16,) + tile, F32),
            pltpu.VMEM((8, 8) + tile, I16),
            pltpu.VMEM((8, 8) + one, F32),
            pltpu.VMEM((8, 8) + tile, I16),
            pltpu.VMEM((8, 8) + one, F32),
            *ring_scratch(4, True),
            *ring_scratch(4, True),
            *ring_scratch(1, True),
            *ring_scratch(1, True),
            *ring_scratch(4, True),
            *ring_scratch(2, False),
            pltpu.VMEM((4, 2) + tile, F32),
            pltpu.VMEM((4, 2) + tile, F32),
            pltpu.VMEM((8,) + tile, F32),
            pltpu.VMEM((8,) + tile, I16),
            pltpu.VMEM((8,) + one, F32),
            pltpu.VMEM((8,) + tile, I16),
            pltpu.VMEM((8,) + one, F32),
            DMA((11,)),
            DMA((96,)),
            DMA((96,)),
            DMA((8,)),
            DMA((8,)),
            DMA((8,)),
            DMA((8,)),
        ],
        compiler_params=remote_params(1),
    )(far, num.reshape(-1, BLK, BLK))


def settle_body(
    idx, live, where, own, hub, halo, num, deg, feats, grads, w_self, w_neigh, bias,
    own_out, relay_out, codes, scales, layer, weights, table, self_rows, code, scale, sem, out_sem,
):
    share = lax.axis_index("esplit")
    step = own.shape[0] // 4
    loads = []
    for g in range(4):
        part = pl.ds(g * step, step)
        loads.append(pltpu.make_async_copy(own.at[part], table.at[part], sem.at[g]))
    first = pl.multiple_of(where[0], 128)
    loads.append(pltpu.make_async_copy(feats.at[pl.ds(first, 512)], self_rows, sem.at[4]))
    for load in loads:
        load.start()

    at = pl.multiple_of(share * 512, 512)
    my_grads = grads[pl.ds(at, 512), :]
    wide = my_grads.astype(F32)
    loads[4].wait()
    mine = self_rows[...]
    contract = (((0,), (0,)), ((), ()))
    weights[0:128, :] = lax.dot_general(mine, my_grads, contract, preferred_element_type=F32)
    neigh = jnp.zeros((128, 128), F32)
    for i in range(4):
        divisor = jnp.maximum(deg[pl.ds(share * 4 + i, 1), :], 1.0)
        aggregate = num[i] / jnp.broadcast_to(divisor, (128, 128)).T
        rows = slice(i * 128, (i + 1) * 128)
        layer[rows, :] = (
            jnp.dot(
                aggregate,
                w_neigh[...].astype(F32),
                precision=lax.Precision.HIGHEST,
                preferred_element_type=F32,
            )
            + jnp.dot(mine[rows], w_self[...], preferred_element_type=F32)
            + bias[...].astype(F32)
        ).astype(BF16)
        neigh = neigh + lax.dot_general(
            aggregate, wide[rows], contract,
            precision=lax.Precision.HIGHEST, preferred_element_type=F32,
        )
    weights[128:256, :] = neigh
    weights[256:264, :] = jnp.broadcast_to(jnp.sum(wide, axis=0, keepdims=True), (8, 128))
    for j in range(8):
        row = lax.broadcasted_iota(I32, (128, 128), 0)
        halo[pl.ds(j * 128, 128), :] = jnp.where(
            row < live[j], halo[pl.ds(j * 128, 128), :], 0.0
        )
    back = lax.dot_general(
        my_grads, w_self[...], (((1,), (1,)), ((), ())), preferred_element_type=F32
    )
    for load in loads[:4]:
        load.wait()
    table[pl.ds(first, 512), :] += back

    def scatter(rows, base, count):
        @pl.loop(0, count // 8)
        def _(g):
            places = [idx[base + g * 8 + i] for i in range(8)]
            values = [
                table[pl.ds(places[i], 1), :] + rows[pl.ds(g * 8 + i, 1), :] for i in range(8)
            ]
            for i in range(8):
                table[pl.ds(places[i], 1), :] = values[i]

    scatter(hub, 0, 512)
    for j in range(8):
        scatter(halo.at[pl.ds(j * 128, 128)], 512 + j * 128, 128)
    outs = []

    def put(src, dst):
        outs.append(pltpu.make_async_copy(src, dst, out_sem.at[len(outs)]))
        outs[-1].start()

    def rows_for(by, half):
        quarter = lax.rem(share + (by + 4), 4)
        return pl.multiple_of((quarter * 2 + half) * 2048, 2048)

    put(table.at[pl.ds(rows_for(0, 0), 4096)], own_out)
    put(table.at[pl.ds(rows_for(1, 0), 2048)], relay_out.at[0])
    put(table.at[pl.ds(rows_for(-1, 1), 2048)], relay_out.at[1])
    for m, by, half in ((0, 2, 0), (1, 2, 1), (2, 1, 1), (3, -1, 0)):
        base = rows_for(by, half)

        @pl.loop(0, 16, unroll=2)
        def _(i):
            rows = pl.ds(pl.multiple_of(base + i * BLK, BLK), BLK)
            code[m, i], scale[m, i] = encode(table[rows, :])

        put(code.at[m], codes.at[m])
        put(scale.at[m], scales.at[m])
    for out in outs:
        out.wait()


def settle(idx, live, where, own, hub, halo, num, deg, feats, grads, w_self, w_neigh, bias):
    codes = (4, 16, BLK, BLK)
    scales = (4, 16, 1, BLK)
    return pl.pallas_call(
        settle_body,
        in_specs=[SMEM, SMEM, SMEM, ANY, VMEM, VMEM, VMEM, VMEM, ANY, VMEM, VMEM, VMEM, VMEM],
        out_specs=[ANY, ANY, ANY, ANY, VMEM, VMEM],
        out_shape=[
            jax.ShapeDtypeStruct((4096, 128), F32),
            jax.ShapeDtypeStruct((2, 2048, 128), F32),
            jax.ShapeDtypeStruct(codes, I16),
            jax.ShapeDtypeStruct(scales, F32),
            jax.ShapeDtypeStruct((512, 128), BF16),
            jax.ShapeDtypeStruct((264, 128), F32),
        ],
        scratch_shapes=[
            pltpu.VMEM(own.shape, F32),
            pltpu.VMEM((512, 128), BF16),
            pltpu.VMEM(codes, I16),
            pltpu.VMEM(scales, F32),
            DMA((5,)),
            DMA((11,)),
        ],
        compiler_params=PARAMS,
    )(idx, live, where, own, hub, halo, num, deg, feats, grads, w_self, w_neigh, bias)


def final_body(
    codes, scales, relay_in, weights, come, come_scale, weights_out,
    far, far_scale, part, out, out_scale, sums, slots, load_sem, send_sem, recv_sem,
):
    place = Place()
    links = Links(send_sem, recv_sem)
    near = [(axis, by) for axis in ("x", "y", "z") for by in (1, -1, 2)] + [("core", 1)]
    ready = greet(place, near)
    loads = [
        pltpu.make_async_copy(relay_in.at[n], part.at[n], load_sem.at[n]) for n in range(2)
    ]
    for load in loads:
        load.start()
    ready()

    def send(m, g, code, scale, to_code, to_scale):
        there = place.device("z", 1 if m % 2 == 0 else -1)
        return [
            links.send(code, to_code, there),
            links.send(scale, to_scale, there),
        ]

    copies = {}
    quad = [pl.ds(g * 4, 4) for g in range(4)]
    for g in range(4):
        for m in (0, 1):
            copies[m, g] = send(
                m, g, codes.at[m, quad[g]], scales.at[m, quad[g]],
                far.at[m, quad[g]], far_scale.at[m, quad[g]],
            )

    def all_sum(stage, axis):
        mine = place.core if axis == "core" else place.at(axis)
        there = [1] if axis == "core" else [1, -1, 2]
        rounds = [
            links.send(sums.at[stage], slots.at[stage, mine], place.device(axis, by))
            for by in there
        ]
        slots[stage, mine] = sums[stage]

        def end():
            for copy in rounds:
                copy.wait_recv()
            total = slots[stage, 0] + slots[stage, 1]
            if axis != "core":
                total = total + (slots[stage, 2] + slots[stage, 3])
            if stage == 3:
                weights_out[...] = total
            else:
                sums[stage + 1] = total

        return end

    sums[0] = weights[...]
    end = all_sum(0, "core")
    for g in range(4):
        for m in (2, 3):
            copies[m, g] = send(
                m, g, codes.at[m, quad[g]], scales.at[m, quad[g]],
                come.at[m - 2, quad[g]], come_scale.at[m - 2, quad[g]],
            )
    for load in loads:
        load.wait()
    for g in range(4):
        for m in (0, 1):
            for copy in copies[m, g]:
                copy.wait_recv()

            @pl.loop(g * 4, g * 4 + 4, unroll=2)
            def _(i):
                block = part[m, i] + decode(far[m, i], far_scale[m, i])
                out[m, i], out_scale[m, i] = encode(block)

            copies[m + 4, g] = send(
                m, g, out.at[m, quad[g]], out_scale.at[m, quad[g]],
                come.at[m + 2, quad[g]], come_scale.at[m + 2, quad[g]],
            )
        end()
        if g < 3:
            end = all_sum(g + 1, ("x", "y", "z")[g])
    for m in (2, 3, 4, 5):
        for g in range(4):
            for copy in copies[m, g]:
                copy.wait_recv()
    links.drain()


def final(codes, scales, relay, weights):
    half = (2, 16, BLK, BLK)
    half_scale = (2, 16, 1, BLK)
    return pl.pallas_call(
        final_body,
        in_specs=[ANY, ANY, ANY, VMEM],
        out_specs=[ANY, ANY, VMEM],
        out_shape=[
            jax.ShapeDtypeStruct((4, 16, BLK, BLK), I16),
            jax.ShapeDtypeStruct((4, 16, 1, BLK), F32),
            jax.ShapeDtypeStruct(weights.shape, F32),
        ],
        scratch_shapes=[
            pltpu.VMEM(half, I16),
            pltpu.VMEM(half_scale, F32),
            pltpu.VMEM(half, F32),
            pltpu.VMEM(half, I16),
            pltpu.VMEM(half_scale, F32),
            pltpu.VMEM((4,) + weights.shape, F32),
            pltpu.VMEM((4, 4) + weights.shape, F32),
            DMA((2,)),
            DMA((64,)),
            DMA((64,)),
        ],
        compiler_params=remote_params(2),
    )(codes, scales, relay.reshape(half), weights)


def total_body(
    own, near, near_scale, relayed, relayed_scale, weights, factor,
    out, w_self_out, w_neigh_out, bias_out,
):
    @pl.loop(0, own.shape[0], unroll=2)
    def _(b):
        others = decode(near[0, b], near_scale[0, b]) + decode(relayed[0, b], relayed_scale[0, b])
        out[b] = own[b] + others

    @pl.when(pl.program_id(0) == 0)
    def _():
        scale = factor[0]
        w_self_out[...] = weights[0:128, :] * scale
        w_neigh_out[...] = weights[128:256, :] * scale
        bias_out[...] = weights[256:257, :] * scale


def total(own, codes, scales, weights, factor):
    def whole(*shape):
        return pl.BlockSpec(shape, lambda i: (0,) * len(shape))

    def message(number):
        return [
            pl.BlockSpec((1, 16, BLK, BLK), lambda i: (number(i), 0, 0, 0)),
            pl.BlockSpec((1, 16, 1, BLK), lambda i: (number(i), 0, 0, 0)),
        ]

    half = pl.BlockSpec((16, BLK, BLK), lambda i: (i, 0, 0))
    return pl.pallas_call(
        total_body,
        grid=(2,),
        in_specs=[
            half,
            *message(lambda i: 1 - i),
            *message(lambda i: 2 + i),
            whole(264, BLK),
            SMEM,
        ],
        out_specs=[half, whole(BLK, BLK), whole(BLK, BLK), whole(1, BLK)],
        out_shape=[
            jax.ShapeDtypeStruct((32, BLK, BLK), F32),
            jax.ShapeDtypeStruct((BLK, BLK), F32),
            jax.ShapeDtypeStruct((BLK, BLK), F32),
            jax.ShapeDtypeStruct((1, BLK), F32),
        ],
        compiler_params=PARAMS,
    )(own, codes, scales, codes, scales, weights, factor)


def local(
    features,
    adjacency,
    tile_source,
    hub_rows,
    send_rows,
    send_live,
    target_block,
    w_self,
    w_neigh,
    out_bias,
    out_grad,
):
    own_count, feat = features.shape
    peers = lax.axis_size("dom")
    d = lax.axis_index("dom")
    z = lax.axis_index("esplit")
    adj = adjacency[0, 0]
    src = tile_source[0, 0]
    blocks, rows, _, cols = adj.shape
    targets = blocks * rows
    hub_idx = hub_rows[0]
    hubs = hub_idx.shape[0]
    share = lax.rem(z - d + peers, 4)
    slots = send_rows.shape[2]
    lists = lax.dynamic_index_in_dim(send_rows[0].reshape(8, 4, slots), share, 1, keepdims=False)
    live = lax.dynamic_index_in_dim(send_live[0].reshape(8, 4), share, 1, keepdims=False)
    idx = jnp.concatenate([hub_idx, lists.reshape(-1)])
    picked = features[idx]
    hub_local = picked[:hubs]
    alive = jnp.arange(slots, dtype=I32)[None, :] < live[:, None]
    halo_local = jnp.where(
        alive[:, :, None], picked[hubs:].reshape(8, slots, feat), jnp.zeros((), features.dtype)
    )
    deg, hub_all, halo_all = exchange(adj, hub_local, halo_local)
    own, far, num = products(
        src,
        adj,
        out_grad,
        w_neigh,
        deg,
        features.reshape(-1, cols, feat),
        hub_all.reshape(-1, cols, feat),
        halo_all.reshape(-1, cols, feat),
    )
    hub_grad, halo_grad, num_sum = owners(far, num)
    where = target_block * rows + z * (targets // 4)
    own, relay, codes, scales, layer, weights = settle(
        idx,
        live,
        where,
        own.reshape(-1, feat),
        hub_grad.reshape(-1, feat),
        halo_grad.reshape(-1, feat),
        num_sum,
        deg,
        features,
        out_grad,
        w_self,
        w_neigh,
        out_bias[None, :],
    )
    codes, scales, weights = final(codes, scales, relay, weights)
    factor = jnp.full((1,), 1.0 / math.sqrt(targets * peers), F32)
    grad_features, self_grad, neigh_grad, bias_grad = total(
        own.reshape(-1, BLK, feat), codes, scales, weights, factor
    )
    return layer, grad_features.reshape(-1, feat), self_grad, neigh_grad, bias_grad[0]


def solution(mesh):
    in_specs = (
        P("dom", None),
        P("dom", "esplit", None, None, None, None),
        P("dom", "esplit", None, None),
        P("dom", None),
        P("dom", None, None),
        P("dom", None),
        P("dom"),
        P(),
        P(),
        P(),
        P("dom", None),
    )
    out_specs = (P(("dom", "esplit"), None), P(("dom", "esplit"), None), P(), P(), P())
    return jax.shard_map(local, mesh=mesh, in_specs=in_specs, out_specs=out_specs, check_vma=False)
```

```python
import functools
import math

import jax
import jax.numpy as jnp
from jax import lax
from jax.experimental import pallas as pl
from jax.experimental.pallas import tpu as pltpu
from jax.sharding import PartitionSpec as P

F32 = jnp.float32
BF16 = jnp.bfloat16
I16 = jnp.int16
I32 = jnp.int32
MESH = pl.DeviceIdType.MESH
DMA = pltpu.SemaphoreType.DMA
VMEM_LIMIT = 56 * 2**20
ANY = pl.BlockSpec(memory_space=pl.ANY)
SMEM = pl.BlockSpec(memory_space=pltpu.SMEM)
VMEM = pl.BlockSpec(memory_space=pltpu.VMEM)
PARAMS = pltpu.CompilerParams(vmem_limit_bytes=VMEM_LIMIT)
BLK = 128
TOP = 32767.0


def remote_params(number):
    return pltpu.CompilerParams(
        vmem_limit_bytes=VMEM_LIMIT, collective_id=number, has_side_effects=True
    )


class Place:
    def __init__(self):
        self.d = lax.axis_index("dom")
        self.z = lax.axis_index("esplit")
        self.core = lax.rem(self.d, 2)
        self.x = lax.rem(lax.div(self.d, 2), 4)
        self.y = lax.div(self.d, 8)

    def at(self, axis):
        return {"x": self.x, "y": self.y, "z": self.z}[axis]

    def step(self, axis, by):
        return lax.rem(self.at(axis) + (by + 4), 4)

    def device(self, axis, by):
        if axis == "core":
            return (self.d + 1 - 2 * self.core, self.z)
        there = self.step(axis, by)
        if axis == "z":
            return (self.d, there)
        if axis == "x":
            return ((self.y * 4 + there) * 2 + self.core, self.z)
        return ((there * 4 + self.x) * 2 + self.core, self.z)

    def share(self):
        return lax.rem(self.z - self.d + 32, 4)


class Links:
    def __init__(self, send_sem, recv_sem):
        self.send_sem, self.recv_sem, self.used, self.made = send_sem, recv_sem, 0, []

    def send(self, src, dst, device):
        assert self.used < self.send_sem.shape[0]
        copy = pltpu.make_async_remote_copy(
            src_ref=src,
            dst_ref=dst,
            send_sem=self.send_sem.at[self.used],
            recv_sem=self.recv_sem.at[self.used],
            device_id=device,
            device_id_type=MESH,
        )
        self.used += 1
        copy.start()
        self.made.append(copy)
        return copy

    def drain(self):
        for copy in self.made:
            copy.wait_send()


def greet(place, near, far=False):
    barrier = pltpu.get_barrier_semaphore()
    for axis, by in near:
        pl.semaphore_signal(
            barrier, inc=1, device_id=place.device(axis, by), device_id_type=MESH
        )
    count = len(near)
    if far:
        share = place.share()
        for j in range(8):
            peer = j * 4 + share

            @pl.when(peer != place.d)
            def _():
                pl.semaphore_signal(
                    barrier, inc=1, device_id=(peer, place.z), device_id_type=MESH
                )

        count = count + 8 - (lax.rem(place.d, 4) == share).astype(I32)

    def wait():
        pl.semaphore_wait(barrier, count)

    return wait


def peer_copy(place, src, dst, j, send_sem, recv_sem, out):
    return pltpu.make_async_remote_copy(
        src_ref=src,
        dst_ref=dst,
        send_sem=send_sem.at[j],
        recv_sem=recv_sem.at[lax.div(place.d, 4) if out else j],
        device_id=(j * 4 + place.share(), place.z),
        device_id_type=MESH,
    )


def block_copy(src, dst, sem, block):
    return pltpu.make_async_copy(src.at[block], dst.at[block], sem.at[block])


def exchange_body(
    hub_idx, list_idx, live, adj, feats, deg_out, hub_out, halo_out,
    buf, packed, wide, picked, hub_in, halo_in, deg_all, deg_mine,
    feat_sem, adj_sem, local_sem, send_sem, recv_sem, far_send, far_recv,
):
    place = Place()
    x, y, c, d, z = place.x, place.y, place.core, place.d, place.z
    share = place.share()
    blocks = adj.shape[0]
    near = [("x", 1), ("x", -1), ("y", 1), ("y", -1), ("z", 1), ("z", -1), ("z", 2), ("core", 1)]
    ready = greet(place, near, far=True)
    span = feats.shape[0] // 4
    feat_copies = []
    for g in range(4):
        part = pl.ds(g * span, span)
        feat_copies.append(pltpu.make_async_copy(feats.at[part], packed.at[part], feat_sem.at[g]))
        feat_copies[-1].start()
    for b in range(blocks):
        block_copy(adj, buf, adj_sem, b).start()
    links = Links(send_sem, recv_sem)
    for g in range(4):
        feat_copies[g].wait()

        @pl.loop(g * span // 128, (g + 1) * span // 128, unroll=2)
        def _(i):
            part = pl.ds(pl.multiple_of(i * 128, 128), 128)
            wide[part, :] = packed[part, :].astype(F32)

    def pick(place_of, store):
        @pl.loop(0, 8)
        def _(g):
            for i in range(16):
                picked[pl.ds(g * 16 + i, 1), :] = wide[pl.ds(place_of(g * 16 + i), 1), :]

        store(picked[...])

    for half in range(2):
        for part in range(2):
            base = (half * 2 + part) * 128

            def store(rows, half=half, part=part):
                hub_in[half, pl.ds(part * 128, 128), :] = rows.astype(BF16)

            pick(lambda i, base=base: hub_idx[base + i], store)
    own_hub = pltpu.make_async_copy(hub_in, hub_out.at[y, x, c], local_sem.at[0])
    own_hub.start()

    def degrees(low, high):
        @pl.loop(low, high)
        def _(b):
            block_copy(adj, buf, adj_sem, b).wait()
            by_column = jnp.sum(buf[b].astype(F32), axis=1)
            rows = lax.dot_general(
                jnp.ones((8, by_column.shape[1]), F32),
                by_column,
                (((1,), (1,)), ((), ())),
                precision=lax.Precision.HIGHEST,
                preferred_element_type=F32,
            )
            deg_mine[pl.ds(b, 1), :] = rows[0:1]

    flows = (("x", "y", 0), ("y", "x", 1))
    cores = []

    def piece(flow, along, across, rows=None):
        axis, other, half = flow
        p, q = place.step(axis, along), place.step(other, across)
        at = (q, p) if axis == "x" else (p, q)
        if rows is None:
            return hub_out.at[at[0], at[1], c, half]
        return hub_out.at[at[0], at[1], c, half, pl.ds(rows * 128, 128)]

    def pass_on(ref, axis, by):
        return links.send(ref, ref, place.device(axis, by))

    def to_core(ref):
        cores.append(pass_on(ref, "core", 1))

    first, relay, second, third = {}, {}, {}, {}
    ready()
    for flow in flows:
        axis, other, half = flow
        for by in (1, -1):
            first[axis, by] = links.send(
                hub_in.at[half], piece(flow, 0, 0), place.device(axis, by)
            )
    for flow in flows:
        axis, other, half = flow
        for by in (1, -1):
            second[axis, 0, by] = links.send(
                hub_in.at[half], piece(flow, 0, 0), place.device(other, by)
            )
    here = lax.div(d, 4)
    for j in range(8):

        def store(rows, j=j):
            slot = lax.broadcasted_iota(I32, rows.shape, 0)
            halo_in[j] = jnp.where(slot < live[j * 4 + share], rows, 0.0).astype(BF16)

        pick(lambda i, j=j: list_idx[j * 4 + share, i], store)

        @pl.when(j * 4 + share != d)
        def _():
            there = halo_out.at[here, lax.rem(d, 4)]
            peer_copy(place, halo_in.at[j], there, j, far_send, far_recv, True).start()

        @pl.when(j * 4 + share == d)
        def _():
            keep = pltpu.make_async_copy(halo_in.at[j], halo_out.at[j, share], local_sem.at[1])
            keep.start()
            keep.wait()

    degrees(0, 4)
    own_hub.wait()
    for flow in flows:
        to_core(piece(flow, 0, 0))
        axis, other, half = flow
        for by, part in ((1, 0), (-1, 1)):
            first[axis, by].wait_recv()
            relay[axis, by] = pass_on(piece(flow, -by, 0, part), axis, by)
        for along in (-1, 1):
            for by in (1, -1):
                second[axis, along, by] = pass_on(piece(flow, along, 0), other, by)
            to_core(piece(flow, along, 0))

    def carry(flow, along):
        axis, other, half = flow
        forward = 1 if along in (0, 2) else -1
        for by in (1, -1):
            second[axis, along, by].wait_recv()
            if by == forward:
                third[axis, along] = pass_on(piece(flow, along, -by), other, by)
            to_core(piece(flow, along, -by))

    degrees(4, 7)
    for flow in flows:
        carry(flow, 0)
    halo_first, halo_relay = {}, []
    for j in range(8):

        @pl.when(j * 4 + share != d)
        def _():
            come = peer_copy(
                place, halo_in.at[j], halo_out.at[j, share], j, far_send, far_recv, False
            )
            come.wait_recv()
            come.wait_send()

        for by in (1, -1):
            halo_first[j, by] = pass_on(halo_out.at[j, share], "z", by)
    for flow in flows:
        axis, other, half = flow
        relay[axis, 1].wait_recv()
        relay[axis, -1].wait_recv()
        for by in (1, -1):
            second[axis, 2, by] = pass_on(piece(flow, 2, 0), other, by)
        to_core(piece(flow, 2, 0))
    degrees(7, blocks)
    deg_all[z] = deg_mine[...]
    deg_copies = [
        links.send(deg_mine, deg_all.at[z], place.device("z", by)) for by in (1, -1, 2)
    ]
    for along in (-1, 1):
        for flow in flows:
            carry(flow, along)
    for j in range(8):
        for by in (1, -1):
            halo_first[j, by].wait_recv()
            if (by == 1) == (j % 2 == 0):
                back = lax.rem(place.step("z", -by) - d + 32, 4)
                halo_relay.append(pass_on(halo_out.at[j, back], "z", by))
    for flow in flows:
        carry(flow, 2)
    for along in (0, -1, 1, 2):
        for flow in flows:
            third[flow[0], along].wait_recv()
            to_core(piece(flow, along, 2))
    for copy in deg_copies:
        copy.wait_recv()
    deg_out[...] = (deg_all[0] + deg_all[1]) + (deg_all[2] + deg_all[3])
    for copy in halo_relay + cores:
        copy.wait_recv()
    links.drain()


def exchange(adj, feats, hub_idx, list_idx, live):
    blocks, rows, _, _ = adj.shape
    hubs, feat = hub_idx.shape[0], feats.shape[1]
    slots = list_idx.shape[1]
    return pl.pallas_call(
        exchange_body,
        in_specs=[SMEM, SMEM, SMEM, ANY, ANY],
        out_specs=[VMEM, ANY, ANY],
        out_shape=[
            jax.ShapeDtypeStruct((blocks, rows), F32),
            jax.ShapeDtypeStruct((4, 4, 2, 2, hubs // 2, feat), BF16),
            jax.ShapeDtypeStruct((8, 4, slots, feat), BF16),
        ],
        scratch_shapes=[
            pltpu.VMEM(adj.shape, BF16),
            pltpu.VMEM(feats.shape, BF16),
            pltpu.VMEM(feats.shape, F32),
            pltpu.VMEM((128, feat), F32),
            pltpu.VMEM((2, hubs // 2, feat), BF16),
            pltpu.VMEM((8, slots, feat), BF16),
            pltpu.VMEM((4, blocks, rows), F32),
            pltpu.VMEM((blocks, rows), F32),
            DMA((4,)),
            DMA((blocks,)),
            DMA((2,)),
            DMA((96,)),
            DMA((96,)),
            DMA((8,)),
            DMA((8,)),
        ],
        compiler_params=remote_params(0),
    )(hub_idx, list_idx, live, adj, feats)


def split_slots(tiles, adj_block):
    rows = adj_block.shape[0]
    for g in range(rows // 16):
        tiles[:, pl.ds(g * 16, 16), :] = jnp.swapaxes(adj_block[pl.ds(g * 16, 16)], 0, 1)


def products_body(
    src, adj, grads, w_neigh, deg, own, hub, halo, own_out, far_out, num,
    table, rows_in, buf, tiles, sem, in_sem, out_sem,
):
    blocks, rows, slots, _ = adj.shape
    for b in range(blocks):
        block_copy(adj, buf, sem, b).start()
    copies = []
    start = 0
    for i, part in enumerate((own, hub, halo)):
        count = part.shape[0]
        copies.append(pltpu.make_async_copy(part, rows_in.at[pl.ds(start, count)], in_sem.at[i]))
        start += count
    for copy in copies:
        copy.start()

    @pl.loop(0, table.shape[0], unroll=8)
    def _(c):
        table[c] = jnp.zeros(table.shape[1:], F32)

    for copy in copies:
        copy.wait()

    @pl.loop(0, blocks)
    def _(b):
        block_copy(adj, buf, sem, b).wait()
        split_slots(tiles, buf.at[b])
        grad_t = lax.dot_general(
            w_neigh[...],
            grads[pl.ds(pl.multiple_of(b * rows, rows), rows), :],
            (((1,), (1,)), ((), ())),
            preferred_element_type=F32,
        )
        grad_t = grad_t / jnp.maximum(deg[pl.ds(b, 1), :], 1.0)
        high = grad_t.astype(BF16)
        low = (grad_t - high.astype(F32)).astype(BF16)
        both = jnp.concatenate([high, low], axis=1)
        total = jnp.zeros((rows, num.shape[1]), F32)
        for k in range(0, slots, 2):
            c0, c1 = src[b, k], src[b, k + 1]
            pair = jnp.concatenate([tiles[k], tiles[k + 1]], axis=1)
            part = jnp.dot(both, jnp.concatenate([pair, pair], axis=0), preferred_element_type=F32)
            table[c0] += part[:, : part.shape[1] // 2]
            table[c1] += part[:, part.shape[1] // 2 :]
            rhs = jnp.concatenate([rows_in[c0], rows_in[c1]], axis=0)
            total = total + jnp.dot(pair, rhs, preferred_element_type=F32)
        num[pl.ds(pl.multiple_of(b * rows, rows), rows), :] = total

    own_blocks = own.shape[0]
    far_blocks = table.shape[0] - own_blocks
    far = pltpu.make_async_copy(table.at[pl.ds(own_blocks, far_blocks)], far_out, out_sem.at[0])
    far.start()
    outs = []
    step = own_blocks // 4
    for g in range(4):

        @pl.loop(g * step, (g + 1) * step, unroll=4)
        def _(c):
            table[c] = table[c].T

        part = pl.ds(g * step, step)
        outs.append(pltpu.make_async_copy(table.at[part], own_out.at[part], out_sem.at[1 + g]))
        outs[-1].start()
    for copy in outs:
        copy.wait()
    far.wait()


def products(src, adj, grads, w_neigh, deg, own, hub, halo):
    blocks, rows, slots, cols = adj.shape
    feat = grads.shape[1]
    far_blocks = hub.shape[0] + halo.shape[0]
    table_blocks = own.shape[0] + far_blocks
    return pl.pallas_call(
        products_body,
        in_specs=[SMEM, ANY, VMEM, VMEM, VMEM, ANY, ANY, ANY],
        out_specs=[ANY, ANY, VMEM],
        out_shape=[
            jax.ShapeDtypeStruct((own.shape[0], cols, feat), F32),
            jax.ShapeDtypeStruct((far_blocks, feat, cols), F32),
            jax.ShapeDtypeStruct((blocks * rows, feat), F32),
        ],
        scratch_shapes=[
            pltpu.VMEM((table_blocks, feat, cols), F32),
            pltpu.VMEM((table_blocks, cols, feat), BF16),
            pltpu.VMEM(adj.shape, BF16),
            pltpu.VMEM((slots, rows, cols), BF16),
            DMA((blocks,)),
            DMA((3,)),
            DMA((5,)),
        ],
        compiler_params=PARAMS,
    )(src, adj, grads, w_neigh, deg, own, hub, halo)


def encode(block):
    top = jnp.maximum(jnp.max(jnp.abs(block), axis=0, keepdims=True), 1e-33)
    return jnp.round(block * (TOP / top)).astype(I32).astype(I16), top * (1.0 / TOP)


def decode(code, scale):
    return code.astype(I32).astype(F32) * scale


class Packet:
    def __init__(self, codes, scales=None):
        self.codes, self.scales = codes, scales

    def put(self, i, block):
        if self.scales is None:
            self.codes[i] = block
        else:
            self.codes[i], self.scales[i] = encode(block)

    def get(self, i):
        if self.scales is None:
            return self.codes[i]
        return decode(self.codes[i], self.scales[i])

    def send(self, links, there, device):
        copies = [links.send(self.codes, there.codes, device)]
        if self.scales is not None:
            copies.append(links.send(self.scales, there.scales, device))
        return copies


class RingSum:
    def __init__(self, place, links, axis, count, load, out_bufs, in_bufs):
        self.place, self.links, self.axis, self.count, self.load = place, links, axis, count, load
        self.out = [Packet(*[ref.at[m] for ref in out_bufs]) for m in range(6)]
        self.come = [Packet(*[ref.at[m] for ref in in_bufs]) for m in range(6)]
        self.copies = {}

    def push(self, m, by, block):
        @pl.loop(0, self.count, unroll=min(2, self.count))
        def _(i):
            self.out[m].put(i, block(i))

        self.copies[m] = self.out[m].send(
            self.links, self.come[m], self.place.device(self.axis, by)
        )

    def wait(self, m):
        for copy in self.copies[m]:
            copy.wait_recv()

    def start_opposite(self):
        there = self.place.step(self.axis, 2)
        for m, by, half in ((0, 1, 0), (1, -1, 1)):
            self.push(m, by, lambda i, half=half: self.load(there, half, i))

    def start_near(self, by):
        m, half = (2, 1) if by == 1 else (3, 0)
        there = self.place.step(self.axis, by)
        self.push(m, by, lambda i: self.load(there, half, i))

    def start(self):
        self.start_opposite()
        self.start_near(1)
        self.start_near(-1)

    def relay(self):
        for m, by, half in ((4, 1, 0), (5, -1, 1)):
            there = self.place.step(self.axis, by)
            self.wait(m - 4)
            self.push(
                m,
                by,
                lambda i, there=there, half=half, m=m: self.load(there, half, i)
                + self.come[m - 4].get(i),
            )

    def finish(self, store):
        here = self.place.at(self.axis)
        for half, a, b in ((0, 4, 3), (1, 5, 2)):
            self.wait(a)
            self.wait(b)

            @pl.loop(0, self.count, unroll=min(2, self.count))
            def _(i):
                store(
                    half,
                    i,
                    self.load(here, half, i) + (self.come[a].get(i) + self.come[b].get(i)),
                )


def ring_scratch(count, coded):
    tile = (6, count, BLK, BLK)
    if not coded:
        return [pltpu.VMEM(tile, F32)] * 2
    pair = [pltpu.VMEM(tile, I16), pltpu.VMEM((6, count, 1, BLK), F32)]
    return pair + pair


def ring_bufs(refs, coded):
    n = 2 if coded else 1
    return refs[:n], refs[n:]


def owners_body(far, num_in, hub_out, halo_out, num_out, mine, theirs, lists, num, *rest):
    (core_out, core_scale_out, core_in, core_scale_in), rest = rest[:4], rest[4:]
    rings = []
    for coded in (True, True, True, True, True, False):
        n = 4 if coded else 2
        rings.append(ring_bufs(rest[:n], coded))
        rest = rest[n:]
    line_x, line_y, list_sum, list_out, list_scale_out, list_in, list_scale_in = rest[:7]
    load_sem, send_sem, recv_sem, far_send, far_recv, far_send2, far_recv2 = rest[7:]
    place = Place()
    x, y, c, d, z = place.x, place.y, place.core, place.d, place.z
    share = place.share()
    links = Links(send_sem, recv_sem)

    near = [("x", 1), ("x", -1), ("y", 1), ("y", -1), ("z", 1), ("z", -1), ("core", 1)]
    ready = greet(place, near, far=True)
    hub_far = far.at[pl.ds(0, 128)].reshape(4, 4, 2, 4, BLK, BLK)

    def part_of(g):
        by = (2, 1, -1, 0)[g // 2]
        if g % 2 == 0:
            return slice(None), place.step("x", by), pl.ds(0, 2)
        return place.step("y", by), slice(None), pl.ds(2, 2)

    def block_at(g, i):
        by = (2, 1, -1, 0)[g // 2]
        if g % 2 == 0:
            return lax.div(i, 2), place.step("x", by), lax.rem(i, 2)
        return place.step("y", by), lax.div(i, 2), 2 + lax.rem(i, 2)

    loads = []

    def load(src, dst):
        loads.append(pltpu.make_async_copy(src, dst, load_sem.at[len(loads)]))
        loads[-1].start()

    for g in range(8):
        p, q, t = part_of(g)
        load(hub_far.at[p, q, 1 - c, t], theirs.at[p, q, t])
    load(far.at[pl.ds(128, 32)], lists)
    load(hub_far.at[:, :, c], mine)
    load(num_in, num)

    def ring(which, axis, count, load):
        return RingSum(place, links, axis, count, load, *rings[which])

    def list_for(there, half, i):
        return lists[(half * 4 + i) * 4 + lax.rem(there - d + 32, 4)]

    list_ring = ring(4, "z", 4, list_for)
    num_ring = ring(5, "z", 2, lambda there, half, i: num[there * 4 + half * 2 + i])
    first_x = ring(0, "x", 4, lambda there, half, i: mine[i, there, half])
    first_y = ring(1, "y", 4, lambda there, half, i: mine[there, i, 2 + half])
    core_copies = []
    there = place.device("core", 1)
    for g in range(8):
        loads[g].wait()

        @pl.loop(0, 8, unroll=2)
        def _(i):
            code, scale = encode(theirs[block_at(g, i)])
            core_out[g, i] = code
            core_scale_out[g, i] = scale

        if g == 0:
            ready()
        core_copies.append(
            [
                links.send(core_out.at[g], core_in.at[g], there),
                links.send(core_scale_out.at[g], core_scale_in.at[g], there),
            ]
        )
        if g == 1:
            loads[8].wait()
            list_ring.start()

    loads[9].wait()

    def merge(g):
        for copy in core_copies[g]:
            copy.wait_recv()

        @pl.loop(0, 8, unroll=2)
        def _(i):
            at = block_at(g, i)
            mine[at] = mine[at] + decode(core_in[g, i], core_scale_in[g, i])

    merge(0)
    first_x.start_opposite()
    merge(1)
    first_y.start_opposite()
    merge(2)
    first_x.start_near(1)
    merge(3)
    first_y.start_near(1)
    merge(4)
    first_x.start_near(-1)
    merge(5)
    first_y.start_near(-1)
    list_ring.relay()
    first_x.relay()
    first_y.relay()
    loads[10].wait()
    num_ring.start()
    merge(6)
    merge(7)

    def keep_list(half, i, total):
        list_sum[half * 4 + i] = total

    list_ring.finish(keep_list)

    @pl.loop(0, 8)
    def _(j):
        code, scale = encode(list_sum[j])
        list_out[j] = code
        list_scale_out[j] = scale

    here = lax.div(d, 4)

    def list_copies(j, out):
        to = here if out else j
        return (
            peer_copy(place, list_out.at[j], list_in.at[to], j, far_send, far_recv, out),
            peer_copy(
                place, list_scale_out.at[j], list_scale_in.at[to], j, far_send2, far_recv2, out
            ),
        )

    for j in range(8):

        @pl.when(j * 4 + share != d)
        def _():
            for copy in list_copies(j, True):
                copy.start()

        @pl.when(j * 4 + share == d)
        def _():
            list_in[j] = list_out[j]
            list_scale_in[j] = list_scale_out[j]

    num_ring.relay()

    def keep_x(half, i, total):
        line_x[i, half] = total

    def keep_y(half, i, total):
        line_y[i, half] = total

    first_x.finish(keep_x)
    first_y.finish(keep_y)
    second_x = ring(2, "y", 1, lambda there, half, i: line_x[there, half])
    second_y = ring(3, "x", 1, lambda there, half, i: line_y[there, half])
    second_x.start()
    second_y.start()

    for j in range(8):

        @pl.when(j * 4 + share != d)
        def _():
            for copy in list_copies(j, False):
                copy.wait_recv()
                copy.wait_send()

        halo_out[j] = decode(list_in[j], list_scale_in[j]).T

    second_x.relay()
    second_y.relay()

    def keep_num(half, i, total):
        num_out[half * 2 + i] = total

    num_ring.finish(keep_num)

    def keep_first(half, i, total):
        hub_out[half] = total.T

    def keep_second(half, i, total):
        hub_out[2 + half] = total.T

    second_x.finish(keep_first)
    second_y.finish(keep_second)
    links.drain()


def owners(far, num):
    tile = (BLK, BLK)
    one = (1, BLK)
    return pl.pallas_call(
        owners_body,
        in_specs=[ANY, ANY],
        out_specs=[VMEM, VMEM, VMEM],
        out_shape=[
            jax.ShapeDtypeStruct((4,) + tile, F32),
            jax.ShapeDtypeStruct((8,) + tile, F32),
            jax.ShapeDtypeStruct((4,) + tile, F32),
        ],
        scratch_shapes=[
            pltpu.VMEM((4, 4, 4) + tile, F32),
            pltpu.VMEM((4, 4, 4) + tile, F32),
            pltpu.VMEM((32,) + tile, F32),
            pltpu.VMEM((16,) + tile, F32),
            pltpu.VMEM((8, 8) + tile, I16),
            pltpu.VMEM((8, 8) + one, F32),
            pltpu.VMEM((8, 8) + tile, I16),
            pltpu.VMEM((8, 8) + one, F32),
            *ring_scratch(4, True),
            *ring_scratch(4, True),
            *ring_scratch(1, True),
            *ring_scratch(1, True),
            *ring_scratch(4, True),
            *ring_scratch(2, False),
            pltpu.VMEM((4, 2) + tile, F32),
            pltpu.VMEM((4, 2) + tile, F32),
            pltpu.VMEM((8,) + tile, F32),
            pltpu.VMEM((8,) + tile, I16),
            pltpu.VMEM((8,) + one, F32),
            pltpu.VMEM((8,) + tile, I16),
            pltpu.VMEM((8,) + one, F32),
            DMA((11,)),
            DMA((96,)),
            DMA((96,)),
            DMA((8,)),
            DMA((8,)),
            DMA((8,)),
            DMA((8,)),
        ],
        compiler_params=remote_params(1),
    )(far, num.reshape(-1, BLK, BLK))


def settle_body(
    hub_idx, list_idx, live, target, own, hub, halo, num, deg, feats, grads, w_self, w_neigh, bias,
    own_out, relay_out, codes, scales, layer, weights, table, self_rows, code, scale, sem, out_sem,
):
    share = lax.axis_index("esplit")
    lists = Place().share()
    step = own.shape[0] // 4
    first = pl.multiple_of(target[0] * 128 + share * 512, 128)
    own_rows = pltpu.make_async_copy(feats.at[pl.ds(first, 512)], self_rows, sem.at[4])
    own_rows.start()
    loads = []
    for g in range(4):
        part = pl.ds(g * step, step)
        loads.append(pltpu.make_async_copy(own.at[part], table.at[part], sem.at[g]))
        loads[-1].start()

    at = pl.multiple_of(share * 512, 512)
    my_grads = grads[pl.ds(at, 512), :]
    wide = my_grads.astype(F32)
    own_rows.wait()
    mine = self_rows[...]
    contract = (((0,), (0,)), ((), ()))
    weights[0:128, :] = lax.dot_general(mine, my_grads, contract, preferred_element_type=F32)
    neigh = jnp.zeros((128, 128), F32)
    for i in range(4):
        divisor = jnp.maximum(deg[pl.ds(share * 4 + i, 1), :], 1.0)
        aggregate = num[i] / jnp.broadcast_to(divisor, (128, 128)).T
        rows = slice(i * 128, (i + 1) * 128)
        layer[rows, :] = (
            jnp.dot(
                aggregate,
                w_neigh[...].astype(F32),
                precision=lax.Precision.HIGHEST,
                preferred_element_type=F32,
            )
            + jnp.dot(mine[rows], w_self[...], preferred_element_type=F32)
            + bias[...].astype(F32)
        ).astype(BF16)
        neigh = neigh + lax.dot_general(
            aggregate, wide[rows], contract,
            precision=lax.Precision.HIGHEST, preferred_element_type=F32,
        )
    weights[128:256, :] = neigh
    weights[256:264, :] = jnp.broadcast_to(jnp.sum(wide, axis=0, keepdims=True), (8, 128))
    weights[264:288, :] = jnp.zeros((24, 128), F32)
    for j in range(8):
        row = lax.broadcasted_iota(I32, (128, 128), 0)
        halo[pl.ds(j * 128, 128), :] = jnp.where(
            row < live[j * 4 + lists], halo[pl.ds(j * 128, 128), :], 0.0
        )
    back = lax.dot_general(
        my_grads, w_self[...], (((1,), (1,)), ((), ())), preferred_element_type=F32
    )
    for load in loads:
        load.wait()
    table[pl.ds(first, 512), :] += back

    def scatter(rows, place_of, count):
        @pl.loop(0, count // 8, unroll=2)
        def _(g):
            places = [place_of(g * 8 + i) for i in range(8)]
            values = [
                table[pl.ds(places[i], 1), :] + rows[pl.ds(g * 8 + i, 1), :] for i in range(8)
            ]
            for i in range(8):
                table[pl.ds(places[i], 1), :] = values[i]

    scatter(hub, lambda i: hub_idx[i], 512)
    for j in range(8):
        scatter(
            halo.at[pl.ds(j * 128, 128)], lambda i, j=j: list_idx[j * 4 + lists, i], 128
        )
    outs = []

    def put(src, dst):
        outs.append(pltpu.make_async_copy(src, dst, out_sem.at[len(outs)]))
        outs[-1].start()

    def rows_for(by, half):
        quarter = lax.rem(share + (by + 4), 4)
        return pl.multiple_of((quarter * 2 + half) * 2048, 2048)

    put(table.at[pl.ds(rows_for(0, 0), 4096)], own_out)
    put(table.at[pl.ds(rows_for(1, 0), 2048)], relay_out.at[0])
    put(table.at[pl.ds(rows_for(-1, 1), 2048)], relay_out.at[1])
    for m, by, half in ((0, 2, 0), (1, 2, 1), (2, 1, 1), (3, -1, 0)):
        base = rows_for(by, half)

        @pl.loop(0, 16, unroll=2)
        def _(i):
            rows = pl.ds(pl.multiple_of(base + i * BLK, BLK), BLK)
            code[m, i], scale[m, i] = encode(table[rows, :])

        put(code.at[m], codes.at[m])
        put(scale.at[m], scales.at[m])
    for out in outs:
        out.wait()


def settle(hub_idx, list_idx, live, target, own, hub, halo, num, deg, feats, grads, w_self, w_neigh, bias):
    codes = (4, 16, BLK, BLK)
    scales = (4, 16, 1, BLK)
    return pl.pallas_call(
        settle_body,
        in_specs=[SMEM, SMEM, SMEM, SMEM, ANY, VMEM, VMEM, VMEM, VMEM, ANY, VMEM, VMEM, VMEM, VMEM],
        out_specs=[ANY, ANY, ANY, ANY, VMEM, VMEM],
        out_shape=[
            jax.ShapeDtypeStruct((4096, 128), F32),
            jax.ShapeDtypeStruct((2, 2048, 128), F32),
            jax.ShapeDtypeStruct(codes, I16),
            jax.ShapeDtypeStruct(scales, F32),
            jax.ShapeDtypeStruct((512, 128), BF16),
            jax.ShapeDtypeStruct((288, 128), F32),
        ],
        scratch_shapes=[
            pltpu.VMEM(own.shape, F32),
            pltpu.VMEM((512, 128), BF16),
            pltpu.VMEM(codes, I16),
            pltpu.VMEM(scales, F32),
            DMA((5,)),
            DMA((11,)),
        ],
        compiler_params=PARAMS,
    )(hub_idx, list_idx, live, target, own, hub, halo, num, deg, feats, grads, w_self, w_neigh, bias)


def final_body(
    codes, scales, relay_in, weights, come, come_scale, weights_out,
    far, far_scale, part, out, out_scale, slots, line, load_sem, send_sem, recv_sem,
):
    place = Place()
    links = Links(send_sem, recv_sem)
    near = [(axis, by) for axis in ("x", "y", "z") for by in (1, -1, 2)] + [("core", 1)]
    ready = greet(place, near)
    loads = [
        pltpu.make_async_copy(relay_in.at[n], part.at[n], load_sem.at[n]) for n in range(2)
    ]
    for load in loads:
        load.start()
    ready()

    def send(m, g, code, scale, to_code, to_scale):
        there = place.device("z", 1 if m % 2 == 0 else -1)
        return [
            links.send(code, to_code, there),
            links.send(scale, to_scale, there),
        ]

    copies = {}
    quad = [pl.ds(g * 4, 4) for g in range(4)]
    for g in range(4):
        for m in (0, 1):
            copies[m, g] = send(
                m, g, codes.at[m, quad[g]], scales.at[m, quad[g]],
                far.at[m, quad[g]], far_scale.at[m, quad[g]],
            )

    x = place.x
    held = {}

    def scatter_sum():
        rounds = [
            links.send(weights.at[place.step("x", by)], slots.at[0, x], place.device("x", by))
            for by in (1, -1, 2)
        ]
        slots[0, x] = weights[x]

        def end():
            for copy in rounds:
                copy.wait_recv()
            held[0] = (slots[0, 0] + slots[0, 1]) + (slots[0, 2] + slots[0, 3])

        return end

    def all_sum(stage, axis):
        mine = place.core if axis == "core" else place.at(axis)
        line[stage - 1] = held[0]
        rounds = [
            links.send(line.at[stage - 1], slots.at[stage, mine], place.device(axis, by))
            for by in ([1] if axis == "core" else [1, -1, 2])
        ]
        slots[stage, mine] = held[0]

        def end():
            for copy in rounds:
                copy.wait_recv()
            total = slots[stage, 0] + slots[stage, 1]
            if axis != "core":
                total = total + (slots[stage, 2] + slots[stage, 3])
            held[0] = total

        return end

    def gather_parts():
        line[3] = held[0]
        rounds = [
            links.send(line.at[3], weights_out.at[x], place.device("x", by)) for by in (1, -1, 2)
        ]
        weights_out[x] = held[0]

        def end():
            for copy in rounds:
                copy.wait_recv()

        return end

    end = scatter_sum()
    for g in range(4):
        for m in (2, 3):
            copies[m, g] = send(
                m, g, codes.at[m, quad[g]], scales.at[m, quad[g]],
                come.at[m - 2, quad[g]], come_scale.at[m - 2, quad[g]],
            )
    for load in loads:
        load.wait()
    for g in range(4):
        for m in (0, 1):
            for copy in copies[m, g]:
                copy.wait_recv()

            @pl.loop(g * 4, g * 4 + 4, unroll=2)
            def _(i):
                block = part[m, i] + decode(far[m, i], far_scale[m, i])
                out[m, i], out_scale[m, i] = encode(block)

            copies[m + 4, g] = send(
                m, g, out.at[m, quad[g]], out_scale.at[m, quad[g]],
                come.at[m + 2, quad[g]], come_scale.at[m + 2, quad[g]],
            )
        end()
        if g < 3:
            end = all_sum(g + 1, ("y", "core", "z")[g])
        else:
            end = gather_parts()
    end()
    for m in (2, 3, 4, 5):
        for g in range(4):
            for copy in copies[m, g]:
                copy.wait_recv()
    links.drain()


def final(codes, scales, relay, weights):
    half = (2, 16, BLK, BLK)
    half_scale = (2, 16, 1, BLK)
    return pl.pallas_call(
        final_body,
        in_specs=[ANY, ANY, ANY, VMEM],
        out_specs=[ANY, ANY, VMEM],
        out_shape=[
            jax.ShapeDtypeStruct((4, 16, BLK, BLK), I16),
            jax.ShapeDtypeStruct((4, 16, 1, BLK), F32),
            jax.ShapeDtypeStruct(weights.shape, F32),
        ],
        scratch_shapes=[
            pltpu.VMEM(half, I16),
            pltpu.VMEM(half_scale, F32),
            pltpu.VMEM(half, F32),
            pltpu.VMEM(half, I16),
            pltpu.VMEM(half_scale, F32),
            pltpu.VMEM((4,) + weights.shape, F32),
            pltpu.VMEM(weights.shape, F32),
            DMA((2,)),
            DMA((64,)),
            DMA((64,)),
        ],
        compiler_params=remote_params(2),
    )(codes, scales, relay.reshape(half), weights)


def total_body(
    factor, own, near, near_scale, relayed, relayed_scale, weights,
    out, w_self_out, w_neigh_out, bias_out,
):
    @pl.loop(0, own.shape[0], unroll=2)
    def _(b):
        others = decode(near[0, b], near_scale[0, b]) + decode(relayed[0, b], relayed_scale[0, b])
        out[b] = own[b] + others

    @pl.when(pl.program_id(0) == 0)
    def _():
        w_self_out[...] = weights[0:128, :] * factor
        w_neigh_out[...] = weights[128:256, :] * factor
        bias_out[...] = weights[256:257, :] * factor


def total(own, codes, scales, weights, factor):
    def whole(*shape):
        return pl.BlockSpec(shape, lambda i: (0,) * len(shape))

    def message(number):
        return [
            pl.BlockSpec((1, 16, BLK, BLK), lambda i: (number(i), 0, 0, 0)),
            pl.BlockSpec((1, 16, 1, BLK), lambda i: (number(i), 0, 0, 0)),
        ]

    half = pl.BlockSpec((16, BLK, BLK), lambda i: (i, 0, 0))
    return pl.pallas_call(
        functools.partial(total_body, factor),
        grid=(2,),
        in_specs=[
            half,
            *message(lambda i: 1 - i),
            *message(lambda i: 2 + i),
            whole(288, BLK),
        ],
        out_specs=[half, whole(BLK, BLK), whole(BLK, BLK), whole(1, BLK)],
        out_shape=[
            jax.ShapeDtypeStruct((32, BLK, BLK), F32),
            jax.ShapeDtypeStruct((BLK, BLK), F32),
            jax.ShapeDtypeStruct((BLK, BLK), F32),
            jax.ShapeDtypeStruct((1, BLK), F32),
        ],
        compiler_params=PARAMS,
    )(own, codes, scales, codes, scales, weights)


def local(
    features,
    adjacency,
    tile_source,
    hub_rows,
    send_rows,
    send_live,
    target_block,
    w_self,
    w_neigh,
    out_bias,
    out_grad,
):
    own_count, feat = features.shape
    peers = lax.axis_size("dom")
    adj = adjacency[0, 0]
    src = tile_source[0, 0]
    blocks, rows, _, cols = adj.shape
    targets = blocks * rows
    hub_idx, list_idx, live = hub_rows[0], send_rows[0], send_live[0]
    deg, hub_all, halo_all = exchange(adj, features, hub_idx, list_idx, live)
    own, far, num = products(
        src,
        adj,
        out_grad,
        w_neigh,
        deg,
        features.reshape(-1, cols, feat),
        hub_all.reshape(-1, cols, feat),
        halo_all.reshape(-1, cols, feat),
    )
    hub_grad, halo_grad, num_sum = owners(far, num)
    own, relay, codes, scales, layer, weights = settle(
        hub_idx,
        list_idx,
        live,
        target_block,
        own.reshape(-1, feat),
        hub_grad.reshape(-1, feat),
        halo_grad.reshape(-1, feat),
        num_sum,
        deg,
        features,
        out_grad,
        w_self,
        w_neigh,
        out_bias[None, :],
    )
    codes, scales, weights = final(codes, scales, relay, weights.reshape(4, 72, feat))
    weights = weights.reshape(-1, feat)
    factor = 1.0 / math.sqrt(targets * peers)
    grad_features, self_grad, neigh_grad, bias_grad = total(
        own.reshape(-1, BLK, feat), codes, scales, weights, factor
    )
    return layer, grad_features.reshape(-1, feat), self_grad, neigh_grad, bias_grad[0]


def solution(mesh):
    in_specs = (
        P("dom", None),
        P("dom", "esplit", None, None, None, None),
        P("dom", "esplit", None, None),
        P("dom", None),
        P("dom", None, None),
        P("dom", None),
        P("dom"),
        P(),
        P(),
        P(),
        P("dom", None),
    )
    out_specs = (P(("dom", "esplit"), None), P(("dom", "esplit"), None), P(), P(), P())
    return jax.shard_map(local, mesh=mesh, in_specs=in_specs, out_specs=out_specs, check_vma=False)
```

```python
import functools
import math

import jax
import jax.numpy as jnp
from jax import lax
from jax.experimental import pallas as pl
from jax.experimental.pallas import tpu as pltpu
from jax.sharding import PartitionSpec as P

F32 = jnp.float32
BF16 = jnp.bfloat16
I16 = jnp.int16
I32 = jnp.int32
MESH = pl.DeviceIdType.MESH
DMA = pltpu.SemaphoreType.DMA
VMEM_LIMIT = 56 * 2**20
ANY = pl.BlockSpec(memory_space=pl.ANY)
SMEM = pl.BlockSpec(memory_space=pltpu.SMEM)
VMEM = pl.BlockSpec(memory_space=pltpu.VMEM)
PARAMS = pltpu.CompilerParams(vmem_limit_bytes=VMEM_LIMIT)
BLK = 128
TOP = 32767.0


def remote_params(number):
    return pltpu.CompilerParams(
        vmem_limit_bytes=VMEM_LIMIT, collective_id=number, has_side_effects=True
    )


class Place:
    def __init__(self):
        self.d = lax.axis_index("dom")
        self.z = lax.axis_index("esplit")
        self.core = lax.rem(self.d, 2)
        self.x = lax.rem(lax.div(self.d, 2), 4)
        self.y = lax.div(self.d, 8)

    def at(self, axis):
        return {"x": self.x, "y": self.y, "z": self.z}[axis]

    def step(self, axis, by):
        return lax.rem(self.at(axis) + (by + 4), 4)

    def device(self, axis, by):
        if axis == "core":
            return (self.d + 1 - 2 * self.core, self.z)
        there = self.step(axis, by)
        if axis == "z":
            return (self.d, there)
        if axis == "x":
            return ((self.y * 4 + there) * 2 + self.core, self.z)
        return ((there * 4 + self.x) * 2 + self.core, self.z)

    def share(self):
        return lax.rem(self.z - self.d + 32, 4)


class Links:
    def __init__(self, send_sem, recv_sem):
        self.send_sem, self.recv_sem, self.used, self.made = send_sem, recv_sem, 0, []

    def send(self, src, dst, device):
        assert self.used < self.send_sem.shape[0]
        copy = pltpu.make_async_remote_copy(
            src_ref=src,
            dst_ref=dst,
            send_sem=self.send_sem.at[self.used],
            recv_sem=self.recv_sem.at[self.used],
            device_id=device,
            device_id_type=MESH,
        )
        self.used += 1
        copy.start()
        self.made.append(copy)
        return copy

    def drain(self):
        for copy in self.made:
            copy.wait_send()


def greet(place, near, far=False):
    barrier = pltpu.get_barrier_semaphore()
    for axis, by in near:
        pl.semaphore_signal(
            barrier, inc=1, device_id=place.device(axis, by), device_id_type=MESH
        )
    count = len(near)
    if far:
        share = place.share()
        for j in range(8):
            peer = j * 4 + share

            @pl.when(peer != place.d)
            def _():
                pl.semaphore_signal(
                    barrier, inc=1, device_id=(peer, place.z), device_id_type=MESH
                )

        count = count + 8 - (lax.rem(place.d, 4) == share).astype(I32)

    def wait():
        pl.semaphore_wait(barrier, count)

    return wait


def peer_copy(place, src, dst, j, send_sem, recv_sem, out):
    return pltpu.make_async_remote_copy(
        src_ref=src,
        dst_ref=dst,
        send_sem=send_sem.at[j],
        recv_sem=recv_sem.at[lax.div(place.d, 4) if out else j],
        device_id=(j * 4 + place.share(), place.z),
        device_id_type=MESH,
    )


def block_copy(src, dst, sem, block):
    return pltpu.make_async_copy(src.at[block], dst.at[block], sem.at[block])


def exchange_body(
    hub_idx, list_idx, live, adj, feats, deg_out, hub_out, halo_out,
    buf, packed, wide, picked, hub_in, halo_in, deg_all, deg_mine,
    feat_sem, adj_sem, local_sem, send_sem, recv_sem, far_send, far_recv,
):
    place = Place()
    x, y, c, d, z = place.x, place.y, place.core, place.d, place.z
    share = place.share()
    blocks = adj.shape[0]
    near = [("x", 1), ("x", -1), ("y", 1), ("y", -1), ("z", 1), ("z", -1), ("z", 2), ("core", 1)]
    ready = greet(place, near, far=True)
    span = feats.shape[0] // 4
    feat_copies = []
    for g in range(4):
        part = pl.ds(g * span, span)
        feat_copies.append(pltpu.make_async_copy(feats.at[part], packed.at[part], feat_sem.at[g]))
        feat_copies[-1].start()
    for b in range(blocks):
        block_copy(adj, buf, adj_sem, b).start()
    links = Links(send_sem, recv_sem)
    for g in range(4):
        feat_copies[g].wait()

        @pl.loop(g * span // 128, (g + 1) * span // 128, unroll=2)
        def _(i):
            part = pl.ds(pl.multiple_of(i * 128, 128), 128)
            wide[part, :] = packed[part, :].astype(F32)

    def pick(place_of, store):
        @pl.loop(0, 8)
        def _(g):
            for i in range(16):
                picked[pl.ds(g * 16 + i, 1), :] = wide[pl.ds(place_of(g * 16 + i), 1), :]

        store(picked[...])

    for half in range(2):
        for part in range(2):
            base = (half * 2 + part) * 128

            def store(rows, half=half, part=part):
                hub_in[half, pl.ds(part * 128, 128), :] = rows.astype(BF16)

            pick(lambda i, base=base: hub_idx[base + i], store)
    own_hub = pltpu.make_async_copy(hub_in, hub_out.at[y, x, c], local_sem.at[0])
    own_hub.start()

    def degrees(low, high):
        @pl.loop(low, high)
        def _(b):
            block_copy(adj, buf, adj_sem, b).wait()
            by_column = jnp.sum(buf[b].astype(F32), axis=1)
            rows = lax.dot_general(
                jnp.ones((8, by_column.shape[1]), F32),
                by_column,
                (((1,), (1,)), ((), ())),
                precision=lax.Precision.HIGHEST,
                preferred_element_type=F32,
            )
            deg_mine[pl.ds(b, 1), :] = rows[0:1]

    flows = (("x", "y", 0), ("y", "x", 1))
    cores = []

    def piece(flow, along, across, rows=None):
        axis, other, half = flow
        p, q = place.step(axis, along), place.step(other, across)
        at = (q, p) if axis == "x" else (p, q)
        if rows is None:
            return hub_out.at[at[0], at[1], c, half]
        return hub_out.at[at[0], at[1], c, half, pl.ds(rows * 128, 128)]

    def pass_on(ref, axis, by):
        return links.send(ref, ref, place.device(axis, by))

    def to_core(ref):
        cores.append(pass_on(ref, "core", 1))

    first, relay, second, third = {}, {}, {}, {}
    ready()
    for flow in flows:
        axis, other, half = flow
        for by in (1, -1):
            first[axis, by] = links.send(
                hub_in.at[half], piece(flow, 0, 0), place.device(axis, by)
            )
    for flow in flows:
        axis, other, half = flow
        for by in (1, -1):
            second[axis, 0, by] = links.send(
                hub_in.at[half], piece(flow, 0, 0), place.device(other, by)
            )
    here = lax.div(d, 4)
    for j in range(8):

        def store(rows, j=j):
            slot = lax.broadcasted_iota(I32, rows.shape, 0)
            halo_in[j] = jnp.where(slot < live[j * 4 + share], rows, 0.0).astype(BF16)

        pick(lambda i, j=j: list_idx[j * 4 + share, i], store)

        @pl.when(j * 4 + share != d)
        def _():
            there = halo_out.at[here, lax.rem(d, 4)]
            peer_copy(place, halo_in.at[j], there, j, far_send, far_recv, True).start()

        @pl.when(j * 4 + share == d)
        def _():
            keep = pltpu.make_async_copy(halo_in.at[j], halo_out.at[j, share], local_sem.at[1])
            keep.start()
            keep.wait()

    degrees(0, 4)
    own_hub.wait()
    for flow in flows:
        to_core(piece(flow, 0, 0))
        axis, other, half = flow
        for by, part in ((1, 0), (-1, 1)):
            first[axis, by].wait_recv()
            relay[axis, by] = pass_on(piece(flow, -by, 0, part), axis, by)
        for along in (-1, 1):
            for by in (1, -1):
                second[axis, along, by] = pass_on(piece(flow, along, 0), other, by)
            to_core(piece(flow, along, 0))

    def carry(flow, along):
        axis, other, half = flow
        forward = 1 if along in (0, 2) else -1
        for by in (1, -1):
            second[axis, along, by].wait_recv()
            if by == forward:
                third[axis, along] = pass_on(piece(flow, along, -by), other, by)
            to_core(piece(flow, along, -by))

    degrees(4, 7)
    for flow in flows:
        carry(flow, 0)
    halo_first, halo_relay = {}, []
    for j in range(8):

        @pl.when(j * 4 + share != d)
        def _():
            come = peer_copy(
                place, halo_in.at[j], halo_out.at[j, share], j, far_send, far_recv, False
            )
            come.wait_recv()
            come.wait_send()

        for by in (1, -1):
            halo_first[j, by] = pass_on(halo_out.at[j, share], "z", by)
    for flow in flows:
        axis, other, half = flow
        relay[axis, 1].wait_recv()
        relay[axis, -1].wait_recv()
        for by in (1, -1):
            second[axis, 2, by] = pass_on(piece(flow, 2, 0), other, by)
        to_core(piece(flow, 2, 0))
    degrees(7, blocks)
    deg_all[z] = deg_mine[...]
    deg_copies = [
        links.send(deg_mine, deg_all.at[z], place.device("z", by)) for by in (1, -1, 2)
    ]
    for along in (-1, 1):
        for flow in flows:
            carry(flow, along)
    for flow in flows:
        carry(flow, 2)
    for j in range(8):
        for by in (1, -1):
            halo_first[j, by].wait_recv()
            if (by == 1) == (j % 2 == 0):
                back = lax.rem(place.step("z", -by) - d + 32, 4)
                halo_relay.append(pass_on(halo_out.at[j, back], "z", by))
    for along in (0, -1, 1, 2):
        for flow in flows:
            third[flow[0], along].wait_recv()
            to_core(piece(flow, along, 2))
    for copy in deg_copies:
        copy.wait_recv()
    deg_out[...] = (deg_all[0] + deg_all[1]) + (deg_all[2] + deg_all[3])
    for copy in halo_relay + cores:
        copy.wait_recv()
    links.drain()


def exchange(adj, feats, hub_idx, list_idx, live):
    blocks, rows, _, _ = adj.shape
    hubs, feat = hub_idx.shape[0], feats.shape[1]
    slots = list_idx.shape[1]
    return pl.pallas_call(
        exchange_body,
        in_specs=[SMEM, SMEM, SMEM, ANY, ANY],
        out_specs=[VMEM, ANY, ANY],
        out_shape=[
            jax.ShapeDtypeStruct((blocks, rows), F32),
            jax.ShapeDtypeStruct((4, 4, 2, 2, hubs // 2, feat), BF16),
            jax.ShapeDtypeStruct((8, 4, slots, feat), BF16),
        ],
        scratch_shapes=[
            pltpu.VMEM(adj.shape, BF16),
            pltpu.VMEM(feats.shape, BF16),
            pltpu.VMEM(feats.shape, F32),
            pltpu.VMEM((128, feat), F32),
            pltpu.VMEM((2, hubs // 2, feat), BF16),
            pltpu.VMEM((8, slots, feat), BF16),
            pltpu.VMEM((4, blocks, rows), F32),
            pltpu.VMEM((blocks, rows), F32),
            DMA((4,)),
            DMA((blocks,)),
            DMA((2,)),
            DMA((96,)),
            DMA((96,)),
            DMA((8,)),
            DMA((8,)),
        ],
        compiler_params=remote_params(0),
    )(hub_idx, list_idx, live, adj, feats)


def split_slots(tiles, adj_block):
    rows = adj_block.shape[0]
    for g in range(rows // 16):
        tiles[:, pl.ds(g * 16, 16), :] = jnp.swapaxes(adj_block[pl.ds(g * 16, 16)], 0, 1)


def products_body(
    src, adj, grads, w_neigh, deg, own, hub, halo, own_out, far_out, num,
    table, rows_in, buf, tiles, sem, in_sem, out_sem,
):
    blocks, rows, slots, _ = adj.shape
    copies = []
    start = 0
    for i, part in enumerate((own, hub, halo)):
        count = part.shape[0]
        copies.append(pltpu.make_async_copy(part, rows_in.at[pl.ds(start, count)], in_sem.at[i]))
        start += count
    for copy in copies:
        copy.start()
    for b in range(blocks):
        block_copy(adj, buf, sem, b).start()

    @pl.loop(0, table.shape[0], unroll=8)
    def _(c):
        table[c] = jnp.zeros(table.shape[1:], F32)

    for copy in copies:
        copy.wait()

    @pl.loop(0, blocks)
    def _(b):
        block_copy(adj, buf, sem, b).wait()
        split_slots(tiles, buf.at[b])
        grad_t = lax.dot_general(
            w_neigh[...],
            grads[pl.ds(pl.multiple_of(b * rows, rows), rows), :],
            (((1,), (1,)), ((), ())),
            preferred_element_type=F32,
        )
        grad_t = grad_t / jnp.maximum(deg[pl.ds(b, 1), :], 1.0)
        high = grad_t.astype(BF16)
        low = (grad_t - high.astype(F32)).astype(BF16)
        both = jnp.concatenate([high, low], axis=1)
        total = jnp.zeros((rows, num.shape[1]), F32)
        for k in range(0, slots, 2):
            c0, c1 = src[b, k], src[b, k + 1]
            pair = jnp.concatenate([tiles[k], tiles[k + 1]], axis=1)
            part = jnp.dot(both, jnp.concatenate([pair, pair], axis=0), preferred_element_type=F32)
            table[c0] += part[:, : part.shape[1] // 2]
            table[c1] += part[:, part.shape[1] // 2 :]
            rhs = jnp.concatenate([rows_in[c0], rows_in[c1]], axis=0)
            total = total + jnp.dot(pair, rhs, preferred_element_type=F32)
        num[pl.ds(pl.multiple_of(b * rows, rows), rows), :] = total

    own_blocks = own.shape[0]
    far_blocks = table.shape[0] - own_blocks
    far = pltpu.make_async_copy(table.at[pl.ds(own_blocks, far_blocks)], far_out, out_sem.at[0])
    far.start()
    outs = []
    step = own_blocks // 4
    for g in range(4):

        @pl.loop(g * step, (g + 1) * step, unroll=4)
        def _(c):
            table[c] = table[c].T

        part = pl.ds(g * step, step)
        outs.append(pltpu.make_async_copy(table.at[part], own_out.at[part], out_sem.at[1 + g]))
        outs[-1].start()
    for copy in outs:
        copy.wait()
    far.wait()


def products(src, adj, grads, w_neigh, deg, own, hub, halo):
    blocks, rows, slots, cols = adj.shape
    feat = grads.shape[1]
    far_blocks = hub.shape[0] + halo.shape[0]
    table_blocks = own.shape[0] + far_blocks
    return pl.pallas_call(
        products_body,
        in_specs=[SMEM, ANY, VMEM, VMEM, VMEM, ANY, ANY, ANY],
        out_specs=[ANY, ANY, VMEM],
        out_shape=[
            jax.ShapeDtypeStruct((own.shape[0], cols, feat), F32),
            jax.ShapeDtypeStruct((far_blocks, feat, cols), F32),
            jax.ShapeDtypeStruct((blocks * rows, feat), F32),
        ],
        scratch_shapes=[
            pltpu.VMEM((table_blocks, feat, cols), F32),
            pltpu.VMEM((table_blocks, cols, feat), BF16),
            pltpu.VMEM(adj.shape, BF16),
            pltpu.VMEM((slots, rows, cols), BF16),
            DMA((blocks,)),
            DMA((3,)),
            DMA((5,)),
        ],
        compiler_params=PARAMS,
    )(src, adj, grads, w_neigh, deg, own, hub, halo)


def encode(block):
    top = jnp.maximum(jnp.max(jnp.abs(block), axis=0, keepdims=True), 1e-33)
    return jnp.round(block * (TOP / top)).astype(I32).astype(I16), top * (1.0 / TOP)


def decode(code, scale):
    return code.astype(I32).astype(F32) * scale


class Packet:
    def __init__(self, codes, scales=None):
        self.codes, self.scales = codes, scales

    def put(self, i, block):
        if self.scales is None:
            self.codes[i] = block
        else:
            self.codes[i], self.scales[i] = encode(block)

    def get(self, i):
        if self.scales is None:
            return self.codes[i]
        return decode(self.codes[i], self.scales[i])

    def send(self, links, there, device):
        copies = [links.send(self.codes, there.codes, device)]
        if self.scales is not None:
            copies.append(links.send(self.scales, there.scales, device))
        return copies


class RingSum:
    def __init__(self, place, links, axis, count, load, out_bufs, in_bufs):
        self.place, self.links, self.axis, self.count, self.load = place, links, axis, count, load
        self.out = [Packet(*[ref.at[m] for ref in out_bufs]) for m in range(6)]
        self.come = [Packet(*[ref.at[m] for ref in in_bufs]) for m in range(6)]
        self.copies = {}

    def push(self, m, by, block):
        @pl.loop(0, self.count, unroll=min(2, self.count))
        def _(i):
            self.out[m].put(i, block(i))

        self.copies[m] = self.out[m].send(
            self.links, self.come[m], self.place.device(self.axis, by)
        )

    def wait(self, m):
        for copy in self.copies[m]:
            copy.wait_recv()

    def start_opposite(self):
        there = self.place.step(self.axis, 2)
        for m, by, half in ((0, 1, 0), (1, -1, 1)):
            self.push(m, by, lambda i, half=half: self.load(there, half, i))

    def start_near(self, by):
        m, half = (2, 1) if by == 1 else (3, 0)
        there = self.place.step(self.axis, by)
        self.push(m, by, lambda i: self.load(there, half, i))

    def start(self):
        self.start_opposite()
        self.start_near(1)
        self.start_near(-1)

    def relay(self):
        for m, by, half in ((4, 1, 0), (5, -1, 1)):
            there = self.place.step(self.axis, by)
            self.wait(m - 4)
            self.push(
                m,
                by,
                lambda i, there=there, half=half, m=m: self.load(there, half, i)
                + self.come[m - 4].get(i),
            )

    def finish(self, store):
        here = self.place.at(self.axis)
        for half, a, b in ((0, 4, 3), (1, 5, 2)):
            self.wait(a)
            self.wait(b)

            @pl.loop(0, self.count, unroll=min(2, self.count))
            def _(i):
                store(
                    half,
                    i,
                    self.load(here, half, i) + (self.come[a].get(i) + self.come[b].get(i)),
                )


def ring_scratch(count, coded):
    tile = (6, count, BLK, BLK)
    if not coded:
        return [pltpu.VMEM(tile, F32)] * 2
    pair = [pltpu.VMEM(tile, I16), pltpu.VMEM((6, count, 1, BLK), F32)]
    return pair + pair


def ring_bufs(refs, coded):
    n = 2 if coded else 1
    return refs[:n], refs[n:]


def owners_body(far, num_in, hub_out, halo_out, num_out, mine, theirs, lists, num, *rest):
    (core_out, core_scale_out, core_in, core_scale_in), rest = rest[:4], rest[4:]
    rings = []
    for coded in (True, True, True, True, True, False):
        n = 4 if coded else 2
        rings.append(ring_bufs(rest[:n], coded))
        rest = rest[n:]
    line_x, line_y, list_sum, list_out, list_scale_out, list_in, list_scale_in = rest[:7]
    load_sem, send_sem, recv_sem, far_send, far_recv, far_send2, far_recv2 = rest[7:]
    place = Place()
    x, y, c, d, z = place.x, place.y, place.core, place.d, place.z
    share = place.share()
    links = Links(send_sem, recv_sem)

    near = [("x", 1), ("x", -1), ("y", 1), ("y", -1), ("z", 1), ("z", -1), ("core", 1)]
    ready = greet(place, near, far=True)
    hub_far = far.at[pl.ds(0, 128)].reshape(4, 4, 2, 4, BLK, BLK)

    def part_of(g):
        by = (2, 1, -1, 0)[g // 2]
        if g % 2 == 0:
            return slice(None), place.step("x", by), pl.ds(0, 2)
        return place.step("y", by), slice(None), pl.ds(2, 2)

    def block_at(g, i):
        by = (2, 1, -1, 0)[g // 2]
        if g % 2 == 0:
            return lax.div(i, 2), place.step("x", by), lax.rem(i, 2)
        return place.step("y", by), lax.div(i, 2), 2 + lax.rem(i, 2)

    loads = []

    def load(src, dst):
        loads.append(pltpu.make_async_copy(src, dst, load_sem.at[len(loads)]))
        loads[-1].start()

    for g in range(8):
        p, q, t = part_of(g)
        load(hub_far.at[p, q, 1 - c, t], theirs.at[p, q, t])
    load(far.at[pl.ds(128, 32)], lists)
    load(hub_far.at[:, :, c], mine)
    load(num_in, num)

    def ring(which, axis, count, load):
        return RingSum(place, links, axis, count, load, *rings[which])

    def list_for(there, half, i):
        return lists[(half * 4 + i) * 4 + lax.rem(there - d + 32, 4)]

    list_ring = ring(4, "z", 4, list_for)
    num_ring = ring(5, "z", 2, lambda there, half, i: num[there * 4 + half * 2 + i])
    first_x = ring(0, "x", 4, lambda there, half, i: mine[i, there, half])
    first_y = ring(1, "y", 4, lambda there, half, i: mine[there, i, 2 + half])
    core_copies = []
    there = place.device("core", 1)
    for g in range(8):
        loads[g].wait()

        @pl.loop(0, 8, unroll=2)
        def _(i):
            code, scale = encode(theirs[block_at(g, i)])
            core_out[g, i] = code
            core_scale_out[g, i] = scale

        if g == 0:
            ready()
        core_copies.append(
            [
                links.send(core_out.at[g], core_in.at[g], there),
                links.send(core_scale_out.at[g], core_scale_in.at[g], there),
            ]
        )
        if g == 1:
            loads[8].wait()
            list_ring.start()

    loads[9].wait()

    def merge(g):
        for copy in core_copies[g]:
            copy.wait_recv()

        @pl.loop(0, 8, unroll=2)
        def _(i):
            at = block_at(g, i)
            mine[at] = mine[at] + decode(core_in[g, i], core_scale_in[g, i])

    merge(0)
    first_x.start_opposite()
    merge(1)
    first_y.start_opposite()
    merge(2)
    first_x.start_near(1)
    merge(3)
    first_y.start_near(1)
    merge(4)
    first_x.start_near(-1)
    merge(5)
    first_y.start_near(-1)
    list_ring.relay()
    first_x.relay()
    first_y.relay()
    loads[10].wait()
    num_ring.start()
    merge(6)
    merge(7)

    def keep_list(half, i, total):
        list_sum[half * 4 + i] = total

    list_ring.finish(keep_list)

    @pl.loop(0, 8)
    def _(j):
        code, scale = encode(list_sum[j])
        list_out[j] = code
        list_scale_out[j] = scale

    here = lax.div(d, 4)

    def list_copies(j, out):
        to = here if out else j
        return (
            peer_copy(place, list_out.at[j], list_in.at[to], j, far_send, far_recv, out),
            peer_copy(
                place, list_scale_out.at[j], list_scale_in.at[to], j, far_send2, far_recv2, out
            ),
        )

    for j in range(8):

        @pl.when(j * 4 + share != d)
        def _():
            for copy in list_copies(j, True):
                copy.start()

        @pl.when(j * 4 + share == d)
        def _():
            list_in[j] = list_out[j]
            list_scale_in[j] = list_scale_out[j]

    num_ring.relay()

    def keep_x(half, i, total):
        line_x[i, half] = total

    def keep_y(half, i, total):
        line_y[i, half] = total

    first_x.finish(keep_x)
    first_y.finish(keep_y)
    second_x = ring(2, "y", 1, lambda there, half, i: line_x[there, half])
    second_y = ring(3, "x", 1, lambda there, half, i: line_y[there, half])
    second_x.start()
    second_y.start()

    for j in range(8):

        @pl.when(j * 4 + share != d)
        def _():
            for copy in list_copies(j, False):
                copy.wait_recv()
                copy.wait_send()

        halo_out[j] = decode(list_in[j], list_scale_in[j]).T

    second_x.relay()
    second_y.relay()

    def keep_num(half, i, total):
        num_out[half * 2 + i] = total

    num_ring.finish(keep_num)

    def keep_first(half, i, total):
        hub_out[half] = total.T

    def keep_second(half, i, total):
        hub_out[2 + half] = total.T

    second_x.finish(keep_first)
    second_y.finish(keep_second)
    links.drain()


def owners(far, num):
    tile = (BLK, BLK)
    one = (1, BLK)
    return pl.pallas_call(
        owners_body,
        in_specs=[ANY, ANY],
        out_specs=[VMEM, VMEM, VMEM],
        out_shape=[
            jax.ShapeDtypeStruct((4,) + tile, F32),
            jax.ShapeDtypeStruct((8,) + tile, F32),
            jax.ShapeDtypeStruct((4,) + tile, F32),
        ],
        scratch_shapes=[
            pltpu.VMEM((4, 4, 4) + tile, F32),
            pltpu.VMEM((4, 4, 4) + tile, F32),
            pltpu.VMEM((32,) + tile, F32),
            pltpu.VMEM((16,) + tile, F32),
            pltpu.VMEM((8, 8) + tile, I16),
            pltpu.VMEM((8, 8) + one, F32),
            pltpu.VMEM((8, 8) + tile, I16),
            pltpu.VMEM((8, 8) + one, F32),
            *ring_scratch(4, True),
            *ring_scratch(4, True),
            *ring_scratch(1, True),
            *ring_scratch(1, True),
            *ring_scratch(4, True),
            *ring_scratch(2, False),
            pltpu.VMEM((4, 2) + tile, F32),
            pltpu.VMEM((4, 2) + tile, F32),
            pltpu.VMEM((8,) + tile, F32),
            pltpu.VMEM((8,) + tile, I16),
            pltpu.VMEM((8,) + one, F32),
            pltpu.VMEM((8,) + tile, I16),
            pltpu.VMEM((8,) + one, F32),
            DMA((11,)),
            DMA((96,)),
            DMA((96,)),
            DMA((8,)),
            DMA((8,)),
            DMA((8,)),
            DMA((8,)),
        ],
        compiler_params=remote_params(1),
    )(far, num.reshape(-1, BLK, BLK))


def settle_body(
    hub_idx, list_idx, live, target, own, hub, halo, num, deg, feats, grads, w_self, w_neigh, bias,
    own_out, relay_out, codes, scales, layer, weights, table, self_rows, code, scale, sem, out_sem,
):
    share = lax.axis_index("esplit")
    lists = Place().share()
    step = own.shape[0] // 4
    first = pl.multiple_of(target[0] * 128 + share * 512, 128)
    own_rows = pltpu.make_async_copy(feats.at[pl.ds(first, 512)], self_rows, sem.at[4])
    own_rows.start()
    loads = []
    for g in range(4):
        part = pl.ds(g * step, step)
        loads.append(pltpu.make_async_copy(own.at[part], table.at[part], sem.at[g]))
        loads[-1].start()

    at = pl.multiple_of(share * 512, 512)
    my_grads = grads[pl.ds(at, 512), :]
    wide = my_grads.astype(F32)
    own_rows.wait()
    mine = self_rows[...]
    contract = (((0,), (0,)), ((), ()))
    weights[0:128, :] = lax.dot_general(mine, my_grads, contract, preferred_element_type=F32)
    neigh = jnp.zeros((128, 128), F32)
    for i in range(4):
        divisor = jnp.maximum(deg[pl.ds(share * 4 + i, 1), :], 1.0)
        aggregate = num[i] / jnp.broadcast_to(divisor, (128, 128)).T
        rows = slice(i * 128, (i + 1) * 128)
        layer[rows, :] = (
            jnp.dot(
                aggregate,
                w_neigh[...].astype(F32),
                precision=lax.Precision.HIGHEST,
                preferred_element_type=F32,
            )
            + jnp.dot(mine[rows], w_self[...], preferred_element_type=F32)
            + bias[...].astype(F32)
        ).astype(BF16)
        neigh = neigh + lax.dot_general(
            aggregate, wide[rows], contract,
            precision=lax.Precision.HIGHEST, preferred_element_type=F32,
        )
    weights[128:256, :] = neigh
    weights[256:264, :] = jnp.broadcast_to(jnp.sum(wide, axis=0, keepdims=True), (8, 128))
    weights[264:288, :] = jnp.zeros((24, 128), F32)
    for j in range(8):
        row = lax.broadcasted_iota(I32, (128, 128), 0)
        halo[pl.ds(j * 128, 128), :] = jnp.where(
            row < live[j * 4 + lists], halo[pl.ds(j * 128, 128), :], 0.0
        )
    back = lax.dot_general(
        my_grads, w_self[...], (((1,), (1,)), ((), ())), preferred_element_type=F32
    )
    for load in loads:
        load.wait()
    table[pl.ds(first, 512), :] += back

    def scatter(rows, place_of, count):
        @pl.loop(0, count // 8, unroll=2)
        def _(g):
            places = [place_of(g * 8 + i) for i in range(8)]
            values = [
                table[pl.ds(places[i], 1), :] + rows[pl.ds(g * 8 + i, 1), :] for i in range(8)
            ]
            for i in range(8):
                table[pl.ds(places[i], 1), :] = values[i]

    scatter(hub, lambda i: hub_idx[i], 512)
    for j in range(8):
        scatter(
            halo.at[pl.ds(j * 128, 128)], lambda i, j=j: list_idx[j * 4 + lists, i], 128
        )
    outs = []

    def put(src, dst):
        outs.append(pltpu.make_async_copy(src, dst, out_sem.at[len(outs)]))
        outs[-1].start()

    def rows_for(by, half):
        quarter = lax.rem(share + (by + 4), 4)
        return pl.multiple_of((quarter * 2 + half) * 2048, 2048)

    put(table.at[pl.ds(rows_for(0, 0), 4096)], own_out)
    put(table.at[pl.ds(rows_for(1, 0), 2048)], relay_out.at[0])
    put(table.at[pl.ds(rows_for(-1, 1), 2048)], relay_out.at[1])
    for m, by, half in ((0, 2, 0), (1, 2, 1), (2, 1, 1), (3, -1, 0)):
        base = rows_for(by, half)

        @pl.loop(0, 16, unroll=2)
        def _(i):
            rows = pl.ds(pl.multiple_of(base + i * BLK, BLK), BLK)
            code[m, i], scale[m, i] = encode(table[rows, :])

        put(code.at[m], codes.at[m])
        put(scale.at[m], scales.at[m])
    for out in outs:
        out.wait()


def settle(hub_idx, list_idx, live, target, own, hub, halo, num, deg, feats, grads, w_self, w_neigh, bias):
    codes = (4, 16, BLK, BLK)
    scales = (4, 16, 1, BLK)
    return pl.pallas_call(
        settle_body,
        in_specs=[SMEM, SMEM, SMEM, SMEM, ANY, VMEM, VMEM, VMEM, VMEM, ANY, VMEM, VMEM, VMEM, VMEM],
        out_specs=[ANY, ANY, ANY, ANY, VMEM, VMEM],
        out_shape=[
            jax.ShapeDtypeStruct((4096, 128), F32),
            jax.ShapeDtypeStruct((2, 2048, 128), F32),
            jax.ShapeDtypeStruct(codes, I16),
            jax.ShapeDtypeStruct(scales, F32),
            jax.ShapeDtypeStruct((512, 128), BF16),
            jax.ShapeDtypeStruct((288, 128), F32),
        ],
        scratch_shapes=[
            pltpu.VMEM(own.shape, F32),
            pltpu.VMEM((512, 128), BF16),
            pltpu.VMEM(codes, I16),
            pltpu.VMEM(scales, F32),
            DMA((5,)),
            DMA((11,)),
        ],
        compiler_params=PARAMS,
    )(hub_idx, list_idx, live, target, own, hub, halo, num, deg, feats, grads, w_self, w_neigh, bias)


def final_body(
    codes, scales, relay_in, weights, come, come_scale, weights_out,
    far, far_scale, part, out, out_scale, slots, line, load_sem, send_sem, recv_sem,
):
    place = Place()
    links = Links(send_sem, recv_sem)
    near = [(axis, by) for axis in ("x", "y", "z") for by in (1, -1, 2)] + [("core", 1)]
    ready = greet(place, near)
    loads = [
        pltpu.make_async_copy(relay_in.at[n], part.at[n], load_sem.at[n]) for n in range(2)
    ]
    for load in loads:
        load.start()
    ready()

    def send(m, g, code, scale, to_code, to_scale):
        there = place.device("z", 1 if m % 2 == 0 else -1)
        return [
            links.send(code, to_code, there),
            links.send(scale, to_scale, there),
        ]

    copies = {}
    quad = [pl.ds(g * 4, 4) for g in range(4)]
    for g in range(4):
        for m in (0, 1):
            copies[m, g] = send(
                m, g, codes.at[m, quad[g]], scales.at[m, quad[g]],
                far.at[m, quad[g]], far_scale.at[m, quad[g]],
            )

    x = place.x
    held = {}

    def scatter_sum():
        rounds = [
            links.send(weights.at[place.step("x", by)], slots.at[0, x], place.device("x", by))
            for by in (1, -1, 2)
        ]
        slots[0, x] = weights[x]

        def end():
            for copy in rounds:
                copy.wait_recv()
            held[0] = (slots[0, 0] + slots[0, 1]) + (slots[0, 2] + slots[0, 3])

        return end

    def all_sum(stage, axis):
        mine = place.core if axis == "core" else place.at(axis)
        line[stage - 1] = held[0]
        rounds = [
            links.send(line.at[stage - 1], slots.at[stage, mine], place.device(axis, by))
            for by in ([1] if axis == "core" else [1, -1, 2])
        ]
        slots[stage, mine] = held[0]

        def end():
            for copy in rounds:
                copy.wait_recv()
            total = slots[stage, 0] + slots[stage, 1]
            if axis != "core":
                total = total + (slots[stage, 2] + slots[stage, 3])
            held[0] = total

        return end

    def gather_parts():
        line[3] = held[0]
        rounds = [
            links.send(line.at[3], weights_out.at[x], place.device("x", by)) for by in (1, -1, 2)
        ]
        weights_out[x] = held[0]

        def end():
            for copy in rounds:
                copy.wait_recv()

        return end

    end = scatter_sum()
    for g in range(4):
        for m in (2, 3):
            copies[m, g] = send(
                m, g, codes.at[m, quad[g]], scales.at[m, quad[g]],
                come.at[m - 2, quad[g]], come_scale.at[m - 2, quad[g]],
            )
    for load in loads:
        load.wait()
    for g in range(4):
        for m in (0, 1):
            for copy in copies[m, g]:
                copy.wait_recv()

            @pl.loop(g * 4, g * 4 + 4, unroll=2)
            def _(i):
                block = part[m, i] + decode(far[m, i], far_scale[m, i])
                out[m, i], out_scale[m, i] = encode(block)

            copies[m + 4, g] = send(
                m, g, out.at[m, quad[g]], out_scale.at[m, quad[g]],
                come.at[m + 2, quad[g]], come_scale.at[m + 2, quad[g]],
            )
        end()
        if g < 3:
            end = all_sum(g + 1, ("y", "core", "z")[g])
        else:
            end = gather_parts()
    end()
    for m in (2, 3, 4, 5):
        for g in range(4):
            for copy in copies[m, g]:
                copy.wait_recv()
    links.drain()


def final(codes, scales, relay, weights):
    half = (2, 16, BLK, BLK)
    half_scale = (2, 16, 1, BLK)
    return pl.pallas_call(
        final_body,
        in_specs=[ANY, ANY, ANY, VMEM],
        out_specs=[ANY, ANY, VMEM],
        out_shape=[
            jax.ShapeDtypeStruct((4, 16, BLK, BLK), I16),
            jax.ShapeDtypeStruct((4, 16, 1, BLK), F32),
            jax.ShapeDtypeStruct(weights.shape, F32),
        ],
        scratch_shapes=[
            pltpu.VMEM(half, I16),
            pltpu.VMEM(half_scale, F32),
            pltpu.VMEM(half, F32),
            pltpu.VMEM(half, I16),
            pltpu.VMEM(half_scale, F32),
            pltpu.VMEM((4,) + weights.shape, F32),
            pltpu.VMEM(weights.shape, F32),
            DMA((2,)),
            DMA((64,)),
            DMA((64,)),
        ],
        compiler_params=remote_params(2),
    )(codes, scales, relay.reshape(half), weights)


def total_body(
    factor, own, near, near_scale, relayed, relayed_scale, weights,
    out, w_self_out, w_neigh_out, bias_out,
):
    @pl.loop(0, own.shape[0], unroll=2)
    def _(b):
        others = decode(near[0, b], near_scale[0, b]) + decode(relayed[0, b], relayed_scale[0, b])
        out[b] = own[b] + others

    @pl.when(pl.program_id(0) == 0)
    def _():
        w_self_out[...] = weights[0:128, :] * factor
        w_neigh_out[...] = weights[128:256, :] * factor
        bias_out[...] = weights[256:257, :] * factor


def total(own, codes, scales, weights, factor):
    def whole(*shape):
        return pl.BlockSpec(shape, lambda i: (0,) * len(shape))

    def message(number):
        return [
            pl.BlockSpec((1, 16, BLK, BLK), lambda i: (number(i), 0, 0, 0)),
            pl.BlockSpec((1, 16, 1, BLK), lambda i: (number(i), 0, 0, 0)),
        ]

    half = pl.BlockSpec((16, BLK, BLK), lambda i: (i, 0, 0))
    return pl.pallas_call(
        functools.partial(total_body, factor),
        grid=(2,),
        in_specs=[
            half,
            *message(lambda i: 1 - i),
            *message(lambda i: 2 + i),
            whole(288, BLK),
        ],
        out_specs=[half, whole(BLK, BLK), whole(BLK, BLK), whole(1, BLK)],
        out_shape=[
            jax.ShapeDtypeStruct((32, BLK, BLK), F32),
            jax.ShapeDtypeStruct((BLK, BLK), F32),
            jax.ShapeDtypeStruct((BLK, BLK), F32),
            jax.ShapeDtypeStruct((1, BLK), F32),
        ],
        compiler_params=PARAMS,
    )(own, codes, scales, codes, scales, weights)


def local(
    features,
    adjacency,
    tile_source,
    hub_rows,
    send_rows,
    send_live,
    target_block,
    w_self,
    w_neigh,
    out_bias,
    out_grad,
):
    own_count, feat = features.shape
    peers = lax.axis_size("dom")
    adj = adjacency[0, 0]
    src = tile_source[0, 0]
    blocks, rows, _, cols = adj.shape
    targets = blocks * rows
    hub_idx, list_idx, live = hub_rows[0], send_rows[0], send_live[0]
    deg, hub_all, halo_all = exchange(adj, features, hub_idx, list_idx, live)
    own, far, num = products(
        src,
        adj,
        out_grad,
        w_neigh,
        deg,
        features.reshape(-1, cols, feat),
        hub_all.reshape(-1, cols, feat),
        halo_all.reshape(-1, cols, feat),
    )
    hub_grad, halo_grad, num_sum = owners(far, num)
    own, relay, codes, scales, layer, weights = settle(
        hub_idx,
        list_idx,
        live,
        target_block,
        own.reshape(-1, feat),
        hub_grad.reshape(-1, feat),
        halo_grad.reshape(-1, feat),
        num_sum,
        deg,
        features,
        out_grad,
        w_self,
        w_neigh,
        out_bias[None, :],
    )
    codes, scales, weights = final(codes, scales, relay, weights.reshape(4, 72, feat))
    weights = weights.reshape(-1, feat)
    factor = 1.0 / math.sqrt(targets * peers)
    grad_features, self_grad, neigh_grad, bias_grad = total(
        own.reshape(-1, BLK, feat), codes, scales, weights, factor
    )
    return layer, grad_features.reshape(-1, feat), self_grad, neigh_grad, bias_grad[0]


def solution(mesh):
    in_specs = (
        P("dom", None),
        P("dom", "esplit", None, None, None, None),
        P("dom", "esplit", None, None),
        P("dom", None),
        P("dom", None, None),
        P("dom", None),
        P("dom"),
        P(),
        P(),
        P(),
        P("dom", None),
    )
    out_specs = (P(("dom", "esplit"), None), P(("dom", "esplit"), None), P(), P(), P())
    return jax.shard_map(local, mesh=mesh, in_specs=in_specs, out_specs=out_specs, check_vma=False)
```
